32 devices in a mesh: ent: 8 (over z, y), rel: 4 (over x, core).
Axes of the slice: x: 2, y: 2, z: 4, core: 2. Of those that a mesh axis runs over, the one named last changes fastest.
Arguments:
- entity_rows: bfloat16 [8192, 256], P('ent'), may hold values from -2.5 to 2.5
- request_rows: int32 [8, 8, 32], P('ent'), may hold values from 0 to 1023
- edge_heads: int32 [32768], P(('ent', 'rel')), may hold values from 0 to 1023
- edge_rels: int32 [32768], P(('ent', 'rel')), may hold values from 0 to 7
- edge_tails: int32 [32768], P(('ent', 'rel')), may hold values from 0 to 255
- edge_counts: int32 [32], P(('ent', 'rel')), may hold values from 1 to 1024, 20480 in all
- negative_rows: int32 [8192], P(('ent', 'rel')), may hold values from 0 to 1023
- relation_blocks: bfloat16 [32, 8, 32, 32], P('rel'), may hold values from -1 to 1
Outputs:
- entity_grad: float32 [8192, 256], P('ent')
- relation_grad: float32 [32, 8, 32, 32], P('rel')
The draws below stay inside these ranges and needn't reach their ends.
Inputs may be any that keep to these rules, and one draw needn't show every extreme that they name: Edge slots of bucket b at or past edge_counts[b] are ignored; some bucket is full in every draw.
All inputs are finite; a program needn't handle non-finite values. No bound on the sum of `edge_counts` on one device may be relied on, other than what follows from the above.
Results may differ from the reference program's by a relative error of at most 0.009.
Values may be sent and summed in bfloat16 or wider, within the bound.
A program may use at most 64 MiB of HBM per device.

```python
import math
import jax
import jax.numpy as jnp
import numpy as np
from jax import lax

D = 256
BLOCK = 32
R_DEV = 8
E_DEV = 1024
SLOTS = 32
EDGE_DEV = 1024
NEG = 256
PARTS_SIZE = 8
ENTITIES = 8192
RELATIONS = 32
BUCKETS = 32
EDGES = 32768
NEGS = 8192
N_ENT = 8
N_REL = 4


def touch_ends(entries, stream_key, low, top_value):
    shape = entries.shape
    index_at = [jax.random.randint(jax.random.fold_in(stream_key, axis), (), 0, shape[axis]) for axis in range(len(shape))]
    entries = entries.at[tuple(index_at)].set(low)
    longest = shape.index(max(shape))
    index_at[longest] = (index_at[longest] + 1) % shape[longest]
    return entries.at[tuple(index_at)].set(top_value)


def block_scale(key, dims, pieces, least, high):
    loudness = 1.0
    for dim, parts in pieces:
        steps = jax.random.uniform(jax.random.fold_in(jax.random.fold_in(key, 6), dim), (parts,), jnp.float32, least / len(pieces), high / len(pieces))
        loudness = loudness * jnp.repeat(jnp.exp(steps), dims[dim] // parts).reshape((-1,) + (1,) * (len(dims) - 1 - dim))
    return loudness


def split_up(count, total, reach, slope):
    portions = [(1 << 20) // math.isqrt(rank ** slope) + 1 for rank in range(2, count + 1)]
    surplus, holding = total - reach - (count - 1), [1] * (count - 1)
    while surplus > 0:
        candidates = [i for i in range(count - 1) if holding[i] < reach]
        pool, left = sum([portions[i] for i in candidates]), surplus
        for i in candidates:
            extra = min(reach - holding[i], max(1, left * portions[i] // pool), surplus)
            holding[i] = holding[i] + extra
            surplus = surplus - extra
    return np.array([reach] + holding)


def uneven_parts(rng, number_of, total, reach, skew):
    if number_of == 2:
        one = jax.random.randint(rng, (), max(1, total - reach), min(reach, total - 1) + 1)
        return jnp.stack([one, total - one])
    sizes = jnp.asarray(split_up(number_of, total, reach, skew), jnp.int32)
    couples = (number_of - 1) // 2
    source_of, taker = sizes[1:1 + 2 * couples:2], sizes[2:2 + 2 * couples:2]
    slack = jnp.minimum(source_of - 1, reach - taker)
    moved = jax.random.randint(jax.random.fold_in(rng, 1), (couples,), 0, 1 << 20) % (slack + 1)
    sizes = sizes.at[1:1 + 2 * couples:2].set(source_of - moved).at[2:2 + 2 * couples:2].set(taker + moved)
    return sizes[jax.random.permutation(jax.random.fold_in(rng, 2), number_of)]


def bell_draw(own_key, shape, scale, most, pieces=(), kind=jnp.bfloat16):
    result = scale * jax.random.normal(own_key, shape, jnp.float32)
    if pieces:
        result = result * block_scale(own_key, shape, pieces, -0.22, 0.18)
    return jnp.clip(result, -most, most).astype(kind)


def setup_inputs(seed: int = 0) -> dict:
    splits = jax.random.split(jax.random.key(seed), 9)
    entity_rows = bell_draw(splits[0], (ENTITIES, D), 0.35, 2.5, ((0, 8),))
    request_rows = touch_ends(jax.random.randint(splits[1], (PARTS_SIZE, PARTS_SIZE, SLOTS), 0, E_DEV), jax.random.fold_in(splits[1], 1), 0, E_DEV - 1).astype(jnp.int32)
    edge_heads = touch_ends(jax.random.randint(splits[2], (EDGES,), 0, E_DEV), jax.random.fold_in(splits[2], 1), 0, E_DEV - 1).astype(jnp.int32)
    edge_rels = touch_ends(jax.random.randint(splits[3], (EDGES,), 0, R_DEV), jax.random.fold_in(splits[3], 1), 0, R_DEV - 1).astype(jnp.int32)
    edge_tails = touch_ends(jax.random.randint(splits[4], (EDGES,), 0, PARTS_SIZE * SLOTS), jax.random.fold_in(splits[4], 1), 0, (PARTS_SIZE * SLOTS) - 1).astype(jnp.int32)
    edge_counts = uneven_parts(splits[5], BUCKETS, 5 * BUCKETS * EDGE_DEV // 8, EDGE_DEV, 2).astype(jnp.int32)
    negative_rows = touch_ends(jax.random.randint(splits[6], (NEGS,), 0, E_DEV), jax.random.fold_in(splits[6], 1), 0, E_DEV - 1).astype(jnp.int32)
    relation_blocks = bell_draw(splits[7], (RELATIONS, D // BLOCK, BLOCK, BLOCK), BLOCK ** -0.5, 1.0, ((0, 4),))
    return dict(entity_rows=entity_rows, request_rows=request_rows, edge_heads=edge_heads, edge_rels=edge_rels, edge_tails=edge_tails, edge_counts=edge_counts, negative_rows=negative_rows, relation_blocks=relation_blocks)


def reference(entity_rows, request_rows, edge_heads, edge_rels, edge_tails, edge_counts, negative_rows, relation_blocks):
    block_count = D // BLOCK
    grad_start = jnp.zeros((E_DEV * N_ENT, D), jnp.float32)
    rel_start = jnp.zeros((R_DEV * N_REL, block_count, BLOCK, BLOCK), jnp.float32)

    def bucket_step(running, bucket):
        entity_acc, relation_acc = running
        part_index = bucket // N_REL
        block_index = bucket % N_REL
        row_base = (part_index * E_DEV).astype(jnp.int32)
        source_table = lax.dynamic_slice_in_dim(entity_rows, row_base, E_DEV, 0)
        requests = lax.dynamic_index_in_dim(request_rows, part_index, 0, keepdims=False)
        rows_global = (jnp.arange(N_ENT, dtype=jnp.int32)[:, None] * E_DEV + requests).reshape(-1).astype(jnp.int32)
        fetched = entity_rows[rows_global]
        edge_base = (bucket * EDGE_DEV).astype(jnp.int32)
        head_ids = lax.dynamic_slice_in_dim(edge_heads, edge_base, EDGE_DEV, 0)
        rel_ids = lax.dynamic_slice_in_dim(edge_rels, edge_base, EDGE_DEV, 0)
        tail_ids = lax.dynamic_slice_in_dim(edge_tails, edge_base, EDGE_DEV, 0)
        neg_ids = lax.dynamic_slice_in_dim(negative_rows, (bucket * NEG).astype(jnp.int32), NEG, 0)
        live_count = edge_counts[bucket]
        live_mask = (jnp.arange(EDGE_DEV, dtype=jnp.int32) < live_count).astype(jnp.float32)
        operators = lax.dynamic_slice_in_dim(relation_blocks, (block_index * R_DEV).astype(jnp.int32), R_DEV, 0).astype(jnp.float32)
        head_rows = source_table[head_ids]
        tail_rows = fetched[tail_ids]
        neg_rows = source_table[neg_ids]
        rel_hot = (rel_ids[:, None] == jnp.arange(R_DEV, dtype=jnp.int32)[None, :]).astype(jnp.float32)
        head_split = head_rows.astype(jnp.float32).reshape(EDGE_DEV, block_count, BLOCK)
        proj_all = jnp.einsum('enb,rnbc->renc', head_split, operators)
        projected = jnp.sum(rel_hot.T[:, :, None, None] * proj_all, 0).reshape(EDGE_DEV, D).astype(jnp.bfloat16)
        projected_wide = projected.astype(jnp.float32)
        positive = jnp.sum(projected_wide * tail_rows.astype(jnp.float32), -1)
        negative = jnp.dot(projected, neg_rows.T, preferred_element_type=jnp.float32)
        pos_weight = -live_mask * jax.nn.sigmoid(-positive)
        neg_weight = (live_mask[:, None] * jax.nn.sigmoid(negative) / NEG).astype(jnp.bfloat16)
        grad_proj = (pos_weight[:, None] * tail_rows.astype(jnp.float32) + jnp.dot(neg_weight, neg_rows, preferred_element_type=jnp.float32)).astype(jnp.bfloat16)
        weighted = (pos_weight[:, None] * projected_wide).astype(jnp.bfloat16)
        neg_grad = jnp.dot(neg_weight.T, projected, preferred_element_type=jnp.float32).astype(jnp.bfloat16)
        grad_split = grad_proj.astype(jnp.float32).reshape(EDGE_DEV, block_count, BLOCK)
        back_all = jnp.einsum('enc,rnbc->renb', grad_split, operators)
        head_grad = jnp.sum(rel_hot.T[:, :, None, None] * back_all, 0).reshape(EDGE_DEV, D).astype(jnp.bfloat16)
        slot_grad = jax.ops.segment_sum(weighted.astype(jnp.float32), tail_ids, num_segments=N_ENT * SLOTS)
        entity_acc = entity_acc.at[row_base + head_ids].add(head_grad.astype(jnp.float32))
        entity_acc = entity_acc.at[row_base + neg_ids].add(neg_grad.astype(jnp.float32))
        entity_acc = entity_acc.at[rows_global].add(slot_grad)
        rel_term = jnp.einsum('er,enb,enc->rnbc', rel_hot, head_split, grad_split)
        rel_base = (block_index * R_DEV).astype(jnp.int32)
        current = lax.dynamic_slice_in_dim(relation_acc, rel_base, R_DEV, 0)
        relation_acc = lax.dynamic_update_slice_in_dim(relation_acc, current + rel_term, rel_base, 0)
        return (entity_acc, relation_acc), None

    buckets = jnp.arange(N_ENT * N_REL, dtype=jnp.int32)
    (entity_grad, relation_grad), _ = lax.scan(bucket_step, (grad_start, rel_start), buckets)
    return entity_grad, relation_grad
```

```python
import functools

import jax
import jax.numpy as jnp
from jax import lax
from jax.experimental import pallas as pl
from jax.experimental.pallas import tpu as pltpu
from jax.sharding import PartitionSpec as P

MESH = pl.DeviceIdType.MESH
F32 = jnp.float32
BF16 = jnp.bfloat16
LANES = 128


def iota(shape, axis):
    return lax.broadcasted_iota(jnp.int32, shape, axis)


def hot(mask):
    return jnp.where(mask, 1.0, 0.0).astype(BF16)


def nn(a, b):
    return jnp.dot(a, b, preferred_element_type=F32)


def nt(a, b):
    return lax.dot_general(a, b, (((1,), (1,)), ((), ())), preferred_element_type=F32)


def tn(a, b):
    return lax.dot_general(a, b, (((0,), (0,)), ((), ())), preferred_element_type=F32)


def column(row):
    return jnp.transpose(jnp.broadcast_to(row, (LANES, LANES)))


def each(count, body):
    if count <= 8:
        for step in range(count):
            body(step)
    else:
        lax.fori_loop(0, count, lambda step, _: (body(step), 0)[1], 0)


def kernel(
    dims,
    counts_ref,
    entity_ref,
    request_ref,
    heads_ref,
    rels_ref,
    tails_ref,
    negs_ref,
    blocks_ref,
    sum_a_ref,
    sum_b_ref,
    rel_out_ref,
    request_wide,
    request_send,
    request_recv,
    want_send,
    fetched,
    slot_send,
    scatter_hot,
    grads,
    tail_hot_t,
    codes,
    hot_rows,
    operators,
    operators_t,
    masked_heads,
    masked_grads,
    projected,
    neg_weight,
    neg_rows,
    weighted,
    grad_proj,
    grad_proj_t,
    part_send,
    part_recv,
    own_half,
    rel_send,
    rel_recv,
    rel_own,
    request_sems,
    fetch_sems,
    slot_sems,
    part_sems,
    cross_sems,
    near_sems,
    far_sems,
    rs_sems,
    ag_sems,
):
    n_ent, n_rel = dims
    me, rel = lax.axis_index("ent"), lax.axis_index("rel")
    core, side = rel % 2, rel // 2
    near = side * 2 + (1 - core)
    cross = (1 - side) * 2 + core
    entities, width = entity_ref.shape
    slots = request_ref.shape[2]
    slot_total = n_ent * slots
    edges = heads_ref.shape[0] * LANES
    negs = negs_ref.shape[0] * LANES
    block = blocks_ref.shape[1]
    r_count = blocks_ref.shape[0] // width
    chunk = 256
    chunks = edges // chunk
    per = LANES // slots
    head_bits = (entities - 1).bit_length()
    rel_bits = (r_count - 1).bit_length()
    neg_at, slot_at = edges, edges + negs
    half = entities // 2
    live_count = counts_ref[0]

    barrier = pltpu.get_barrier_semaphore()

    def greet(step):
        pl.semaphore_signal(
            barrier, inc=1, device_id=(lax.rem(me + step + 1, n_ent), rel), device_id_type=MESH
        )

    each(n_ent - 1, greet)
    for partner in (near, cross):
        pl.semaphore_signal(barrier, inc=1, device_id=(me, partner), device_id_type=MESH)

    request_wide[...] = jnp.zeros_like(request_wide)
    request_wide[:, :slots] = request_ref[0]
    base = request_wide[...]
    wide = base
    for q in range(1, per):
        wide = wide + pltpu.roll(base, q * slots, 1)
    for p in range(n_ent):
        request_send[p] = jnp.broadcast_to(wide[p : p + 1], (8, LANES))
    request_recv[me] = request_send[me]

    pl.semaphore_wait(barrier, n_ent + 1)

    def exchange(src, dst, sems, step):
        target = lax.rem(me + step + 1, n_ent)
        return pltpu.make_async_remote_copy(
            src_ref=src.at[target],
            dst_ref=dst.at[me],
            send_sem=sems.at[0, target],
            recv_sem=sems.at[1, me],
            device_id=(target, rel),
            device_id_type=MESH,
        )

    def arrival(dst, sems, step):
        source = lax.rem(me + step + 1, n_ent)
        return pltpu.make_async_remote_copy(
            src_ref=dst.at[source],
            dst_ref=dst.at[source],
            send_sem=sems.at[0, source],
            recv_sem=sems.at[1, source],
            device_id=(source, rel),
            device_id_type=MESH,
        )

    def start_all(src, dst, sems):
        each(n_ent - 1, lambda step: exchange(src, dst, sems, step).start())

    def wait_all(dst, sems):
        each(n_ent - 1, lambda step: arrival(dst, sems, step).wait_recv())

    def drain_all(src, dst, sems):
        each(n_ent - 1, lambda step: exchange(src, dst, sems, step).wait_send())

    start_all(request_send, request_recv, request_sems)

    for k in range(edges // LANES):
        code = heads_ref[k : k + 1] + (
            (rels_ref[k : k + 1] + (tails_ref[k : k + 1] << rel_bits)) << head_bits
        )
        codes[k * LANES : (k + 1) * LANES] = column(code)
    lane = iota((LANES, LANES), 1)
    for k in range(negs // LANES):
        ids = column(negs_ref[k : k + 1])
        for c in range(entities // LANES):
            hot_rows[k * LANES : (k + 1) * LANES, c * LANES : (c + 1) * LANES] = hot(
                ids == lane + c * LANES
            )
    neg_rows[...] = nn(hot_rows[:negs], entity_ref[...]).astype(BF16)

    wait_all(request_recv, request_sems)
    request_rows = []
    lane8 = iota((8, LANES), 1) // slots
    for g in range(n_ent // per):
        row = request_recv[g * per]
        for q in range(1, per):
            row = jnp.where(lane8 == q, request_recv[g * per + q], row)
        row = row[:1]
        request_rows.append(row)
        ids = column(row)
        for c in range(entities // LANES):
            hot_rows[:LANES, c * LANES : (c + 1) * LANES] = hot(ids == lane + c * LANES)
        want_send[g * per : (g + 1) * per] = (
            nn(hot_rows[:LANES], entity_ref[...]).astype(BF16).reshape(per, slots, width)
        )
    fetched[me] = want_send[me]
    start_all(want_send, fetched, fetch_sems)

    spread = hot(iota((block, width), 1) % block == iota((block, width), 0))
    spread_t = hot(iota((width, block), 0) % block == iota((width, block), 1))
    diagonal = iota((width, width), 0) // block == iota((width, width), 1) // block
    for r in range(r_count):
        rows = slice(r * width, (r + 1) * width)
        one = blocks_ref[rows]
        operators[rows] = jnp.where(diagonal, nn(one, spread), 0.0).astype(BF16)
        operators_t[rows] = jnp.where(diagonal, nt(spread_t, one), 0.0).astype(BF16)

    def rel_masks(rows):
        ids = (codes[rows] >> head_bits) & (r_count - 1)
        return [hot(ids == r) for r in range(r_count)]

    def mask_by_rel(source, masks, target, rows):
        for r in range(r_count):
            for c in range(width // LANES):
                at = r * width + c * LANES
                target[rows, at : at + LANES] = source[:, c * LANES : (c + 1) * LANES] * masks[r]

    neg_grad = jnp.zeros((negs, width), F32)
    wide_lane = iota((chunk, LANES), 1)
    for i in range(chunks):
        rows = slice(i * chunk, (i + 1) * chunk)
        ids = codes[rows] & (entities - 1)
        for c in range(entities // LANES):
            hot_rows[:, c * LANES : (c + 1) * LANES] = hot(ids == wide_lane + c * LANES)
        head = nn(hot_rows[...], entity_ref[...]).astype(BF16)
        mask_by_rel(head, rel_masks(rows), masked_heads, rows)
        proj = nn(masked_heads[rows], operators[...]).astype(BF16)
        projected[rows] = proj
        score = nt(proj, neg_rows[...])
        live = iota((chunk, negs), 0) + i * chunk < live_count
        weight = jnp.where(live, jax.nn.sigmoid(score) * (1.0 / negs), 0.0).astype(BF16)
        neg_weight[rows] = weight
        neg_grad = neg_grad + tn(weight, proj)
    grads[neg_at : neg_at + negs] = neg_grad.astype(BF16)

    sub = iota((entities, LANES), 0)
    for k in range(edges // LANES):
        scatter_hot[:, k * LANES : (k + 1) * LANES] = hot(sub == heads_ref[k : k + 1])
    for k in range(negs // LANES):
        at = neg_at + k * LANES
        scatter_hot[:, at : at + LANES] = hot(sub == negs_ref[k : k + 1])
    for k, row in enumerate(request_rows):
        at = slot_at + k * LANES
        scatter_hot[:, at : at + LANES] = hot(sub == row)
    slot_sub = iota((slot_total, LANES), 0)
    for k in range(edges // LANES):
        tail_hot_t[:, k * LANES : (k + 1) * LANES] = hot(slot_sub == tails_ref[k : k + 1])

    wait_all(fetched, fetch_sems)
    table = fetched[...].reshape(slot_total, width)
    for i in range(chunks):
        rows = slice(i * chunk, (i + 1) * chunk)
        ids = codes[rows] >> (head_bits + rel_bits)
        tail_hot = jnp.concatenate(
            [hot(ids == wide_lane + c * LANES) for c in range(slot_total // LANES)], axis=1
        )
        tail = nn(tail_hot, table)
        proj = projected[rows].astype(F32)
        positive = jnp.sum(proj * tail, axis=1, keepdims=True)
        live = iota((chunk, 1), 0) + i * chunk < live_count
        pos_weight = jnp.where(live, -jax.nn.sigmoid(-positive), 0.0)
        weighted[rows] = (pos_weight * proj).astype(BF16)
        grad_proj[rows] = (pos_weight * tail + nn(neg_weight[rows], neg_rows[...])).astype(BF16)
    per_step = min(n_ent, 8)
    for g in range(n_ent // per_step):
        rows = slice(g * per_step * slots, (g + 1) * per_step * slots)
        slot_send[g * per_step : (g + 1) * per_step] = (
            nn(tail_hot_t[rows], weighted[...]).astype(BF16).reshape(per_step, slots, width)
        )
    slot_recv = grads.at[slot_at : slot_at + slot_total]

    def slot_copy(step):
        target = lax.rem(me + step + 1, n_ent)
        return pltpu.make_async_remote_copy(
            src_ref=slot_send.at[target],
            dst_ref=grads.at[pl.ds(pl.multiple_of(slot_at + me * slots, slots), slots)],
            send_sem=slot_sems.at[0, target],
            recv_sem=slot_sems.at[1, me],
            device_id=(target, rel),
            device_id_type=MESH,
        )

    def slot_arrival(step):
        source = lax.rem(me + step + 1, n_ent)
        return pltpu.make_async_remote_copy(
            src_ref=slot_send.at[source],
            dst_ref=grads.at[pl.ds(pl.multiple_of(slot_at + source * slots, slots), slots)],
            send_sem=slot_sems.at[0, source],
            recv_sem=slot_sems.at[1, source],
            device_id=(source, rel),
            device_id_type=MESH,
        )

    each(n_ent - 1, lambda step: slot_copy(step).start())
    grads[pl.ds(pl.multiple_of(slot_at + me * slots, slots), slots)] = slot_send[me]

    for i in range(chunks):
        rows = slice(i * chunk, (i + 1) * chunk)
        mask_by_rel(grad_proj[rows], rel_masks(rows), masked_grads, slice(0, chunk))
        grads[rows] = nn(masked_grads[...], operators_t[...]).astype(BF16)

    each(n_ent - 1, lambda step: slot_arrival(step).wait_recv())

    pieces = half // chunk
    part_copies = []
    for q in range(pieces):
        at = pl.multiple_of((1 - core) * half + q * chunk, chunk)
        part_send[q] = nn(scatter_hot[pl.ds(at, chunk)], grads[...]).astype(BF16)
        copy = pltpu.make_async_remote_copy(
            src_ref=part_send.at[q],
            dst_ref=part_recv.at[q],
            send_sem=part_sems.at[0, q],
            recv_sem=part_sems.at[1, q],
            device_id=(me, near),
            device_id_type=MESH,
        )
        copy.start()
        part_copies.append(copy)
    for q in range(pieces):
        at = pl.multiple_of(core * half + q * chunk, chunk)
        own_half[q] = nn(scatter_hot[pl.ds(at, chunk)], grads[...])
    cross_copies, near_copies = [], []
    for q in range(pieces):
        part_copies[q].wait_recv()
        sum_a_ref[core, q] = (own_half[q] + part_recv[q].astype(F32)).astype(BF16)
        copy = pltpu.make_async_remote_copy(
            src_ref=sum_a_ref.at[core, q],
            dst_ref=sum_b_ref.at[core, q],
            send_sem=cross_sems.at[0, q],
            recv_sem=cross_sems.at[1, q],
            device_id=(me, cross),
            device_id_type=MESH,
        )
        copy.start()
        cross_copies.append(copy)
        copy = pltpu.make_async_remote_copy(
            src_ref=sum_a_ref.at[core, q],
            dst_ref=sum_a_ref.at[core, q],
            send_sem=near_sems.at[0, q],
            recv_sem=near_sems.at[1, q],
            device_id=(me, near),
            device_id_type=MESH,
        )
        copy.start()
        near_copies.append(copy)

    wire = rel_send.dtype
    per_owner = rel_send.shape[1]
    grad_proj_t[...] = jnp.transpose(grad_proj[...])
    block_of_lane = iota((block, width), 1) // block
    step_rows = min(block, per_owner)
    for r in range(r_count):
        outer = nn(grad_proj_t[...], masked_heads[:, r * width : (r + 1) * width])
        small = jnp.zeros((block, width), F32)
        for n in range(width // block):
            small = small + jnp.where(
                block_of_lane == n, outer[n * block : (n + 1) * block], 0.0
            )
        for c in range(width // LANES):
            for t in range(block // step_rows):
                flat = (r * (width // LANES) + c) * block + t * step_rows
                owner, at = flat // per_owner, flat % per_owner
                rel_send[owner, at : at + step_rows] = small[
                    t * step_rows : (t + 1) * step_rows, c * LANES : (c + 1) * LANES
                ].astype(wire)
    start_all(rel_send, rel_recv, rs_sems)
    rel_recv[me] = rel_send[me]

    far_copies = []

    def forward(q):
        cross_copies[q].wait_recv()
        copy = pltpu.make_async_remote_copy(
            src_ref=sum_b_ref.at[core, q],
            dst_ref=sum_b_ref.at[core, q],
            send_sem=far_sems.at[0, q],
            recv_sem=far_sems.at[1, q],
            device_id=(me, near),
            device_id_type=MESH,
        )
        copy.start()
        far_copies.append(copy)

    for q in range(pieces - 1):
        forward(q)
    wait_all(rel_recv, rs_sems)
    total = rel_recv[0].astype(F32)
    for p in range(1, n_ent):
        total = total + rel_recv[p].astype(F32)
    rel_own[...] = total.astype(wire)
    rel_out_ref[me] = rel_own[...]

    def gather_copy(step):
        target = lax.rem(me + step + 1, n_ent)
        return pltpu.make_async_remote_copy(
            src_ref=rel_own,
            dst_ref=rel_out_ref.at[me],
            send_sem=ag_sems.at[0, target],
            recv_sem=ag_sems.at[1, me],
            device_id=(target, rel),
            device_id_type=MESH,
        )

    each(n_ent - 1, lambda step: gather_copy(step).start())
    forward(pieces - 1)

    wait_all(rel_out_ref, ag_sems)
    for copies in (near_copies, far_copies):
        for copy in copies:
            copy.wait_recv()
    drain_all(request_send, request_recv, request_sems)
    drain_all(want_send, fetched, fetch_sems)
    each(n_ent - 1, lambda step: slot_copy(step).wait_send())
    drain_all(rel_send, rel_recv, rs_sems)
    each(n_ent - 1, lambda step: gather_copy(step).wait_send())
    for copies in (part_copies, cross_copies, near_copies, far_copies):
        for copy in copies:
            copy.wait_send()


def local(
    n_ent,
    n_rel,
    entity_rows,
    request_rows,
    edge_heads,
    edge_rels,
    edge_tails,
    edge_counts,
    negative_rows,
    relation_blocks,
):
    entities, width = entity_rows.shape
    slots = request_rows.shape[2]
    slot_total = n_ent * slots
    edges = edge_heads.shape[0]
    negs = negative_rows.shape[0]
    r_count, block_count, block, _ = relation_blocks.shape
    chunk = 256
    pieces = entities // 2 // chunk
    stacked = r_count * width
    flat_rows = stacked * block // LANES
    per_owner = flat_rows // n_ent
    wire = BF16 if per_owner % 16 == 0 else F32
    terms = edges + negs + slot_total
    vmem = pltpu.VMEM
    dma = pltpu.SemaphoreType.DMA
    spec = pl.BlockSpec(memory_space=pltpu.VMEM)
    out_shape = (
        jax.ShapeDtypeStruct((2, pieces, chunk, width), BF16),
        jax.ShapeDtypeStruct((2, pieces, chunk, width), BF16),
        jax.ShapeDtypeStruct((n_ent, per_owner, LANES), wire),
    )
    scratch = [
        vmem((n_ent, LANES), jnp.int32),
        vmem((n_ent, 8, LANES), jnp.int32),
        vmem((n_ent, 8, LANES), jnp.int32),
        vmem((n_ent, slots, width), BF16),
        vmem((n_ent, slots, width), BF16),
        vmem((n_ent, slots, width), BF16),
        vmem((entities, terms), BF16),
        vmem((terms, width), BF16),
        vmem((slot_total, edges), BF16),
        vmem((edges, LANES), jnp.int32),
        vmem((chunk, entities), BF16),
        vmem((stacked, width), BF16),
        vmem((stacked, width), BF16),
        vmem((edges, stacked), BF16),
        vmem((chunk, stacked), BF16),
        vmem((edges, width), BF16),
        vmem((edges, negs), BF16),
        vmem((negs, width), BF16),
        vmem((edges, width), BF16),
        vmem((edges, width), BF16),
        vmem((width, edges), BF16),
        vmem((pieces, chunk, width), BF16),
        vmem((pieces, chunk, width), BF16),
        vmem((pieces, chunk, width), F32),
        vmem((n_ent, per_owner, LANES), wire),
        vmem((n_ent, per_owner, LANES), wire),
        vmem((per_owner, LANES), wire),
        dma((2, n_ent)),
        dma((2, n_ent)),
        dma((2, n_ent)),
        dma((2, pieces)),
        dma((2, pieces)),
        dma((2, pieces)),
        dma((2, pieces)),
        dma((2, n_ent)),
        dma((2, n_ent)),
    ]
    sum_a, sum_b, rel_flat = pl.pallas_call(
        functools.partial(kernel, (n_ent, n_rel)),
        out_shape=out_shape,
        in_specs=[pl.BlockSpec(memory_space=pltpu.SMEM)] + [spec] * 7,
        out_specs=(spec,) * 3,
        scratch_shapes=scratch,
        compiler_params=pltpu.CompilerParams(
            collective_id=0, has_side_effects=True, vmem_limit_bytes=56 * 1024 * 1024
        ),
    )(
        edge_counts,
        entity_rows,
        request_rows,
        edge_heads.reshape(edges // LANES, LANES),
        edge_rels.reshape(edges // LANES, LANES),
        edge_tails.reshape(edges // LANES, LANES),
        negative_rows.reshape(negs // LANES, LANES),
        relation_blocks.reshape(stacked, block),
    )
    entity_grad = (sum_a.astype(F32) + sum_b.astype(F32)).reshape(entities, width)
    relation_grad = (
        rel_flat.astype(F32)
        .reshape(stacked // LANES, block, LANES)
        .transpose(0, 2, 1)
        .reshape(relation_blocks.shape)
    )
    return entity_grad, relation_grad


def solution(mesh):
    in_specs = (
        P("ent", None),
        P("ent", None, None),
        P(("ent", "rel")),
        P(("ent", "rel")),
        P(("ent", "rel")),
        P(("ent", "rel")),
        P(("ent", "rel")),
        P("rel", None, None, None),
    )
    out_specs = (P("ent", None), P("rel", None, None, None))
    body = functools.partial(local, mesh.shape["ent"], mesh.shape["rel"])
    return jax.shard_map(body, mesh=mesh, in_specs=in_specs, out_specs=out_specs, check_vma=False)
```

```python
import functools

import jax
import jax.numpy as jnp
from jax import lax
from jax.experimental import pallas as pl
from jax.experimental.pallas import tpu as pltpu
from jax.sharding import PartitionSpec as P

MESH = pl.DeviceIdType.MESH
F32 = jnp.float32
BF16 = jnp.bfloat16
LANES = 128


def iota(shape, axis):
    return lax.broadcasted_iota(jnp.int32, shape, axis)


def hot(mask):
    return jnp.where(mask, 1.0, 0.0).astype(BF16)


def nn(a, b):
    return jnp.dot(a, b, preferred_element_type=F32)


def nt(a, b):
    return lax.dot_general(a, b, (((1,), (1,)), ((), ())), preferred_element_type=F32)


def tn(a, b):
    return lax.dot_general(a, b, (((0,), (0,)), ((), ())), preferred_element_type=F32)


def column(row):
    return jnp.transpose(jnp.broadcast_to(row, (LANES, LANES)))


def each(count, body):
    if count <= 8:
        for step in range(count):
            body(step)
    else:
        lax.fori_loop(0, count, lambda step, _: (body(step), 0)[1], 0)


def kernel(
    dims,
    counts_ref,
    entity_ref,
    request_ref,
    heads_ref,
    rels_ref,
    tails_ref,
    negs_ref,
    blocks_ref,
    sum_a_ref,
    sum_b_ref,
    rel_out_ref,
    request_wide,
    request_send,
    request_recv,
    want_send,
    fetched,
    slot_send,
    scatter_hot,
    grads,
    tail_hot_t,
    codes,
    hot_rows,
    operators,
    operators_t,
    masked_heads,
    masked_grads,
    projected,
    neg_weight,
    neg_rows,
    weighted,
    grad_proj,
    grad_proj_t,
    part_send,
    part_recv,
    rel_send,
    rel_recv,
    rel_own,
    request_sems,
    fetch_sems,
    slot_sems,
    part_sems,
    cross_sems,
    near_sems,
    far_sems,
    rs_sems,
    ag_sems,
):
    n_ent, n_rel = dims
    me, rel = lax.axis_index("ent"), lax.axis_index("rel")
    core, side = rel % 2, rel // 2
    near = side * 2 + (1 - core)
    cross = (1 - side) * 2 + core
    entities, width = entity_ref.shape
    slots = request_ref.shape[2]
    slot_total = n_ent * slots
    edges = heads_ref.shape[0] * LANES
    negs = negs_ref.shape[0] * LANES
    block = blocks_ref.shape[1]
    r_count = blocks_ref.shape[0] // width
    chunk = 256
    chunks = edges // chunk
    per = LANES // slots
    head_bits = (entities - 1).bit_length()
    rel_bits = (r_count - 1).bit_length()
    neg_at, slot_at = edges, edges + negs
    half = entities // 2
    live_count = counts_ref[0]

    barrier = pltpu.get_barrier_semaphore()

    def greet(step):
        pl.semaphore_signal(
            barrier, inc=1, device_id=(lax.rem(me + step + 1, n_ent), rel), device_id_type=MESH
        )

    each(n_ent - 1, greet)
    for partner in (near, cross):
        pl.semaphore_signal(barrier, inc=1, device_id=(me, partner), device_id_type=MESH)

    request_wide[...] = jnp.zeros_like(request_wide)
    request_wide[:, :slots] = request_ref[0]
    base = request_wide[...]
    wide = base
    for q in range(1, per):
        wide = wide + pltpu.roll(base, q * slots, 1)
    for p in range(n_ent):
        request_send[p] = jnp.broadcast_to(wide[p : p + 1], (8, LANES))
    request_recv[me] = request_send[me]

    for k in range(edges // LANES):
        code = heads_ref[k : k + 1] + (
            (rels_ref[k : k + 1] + (tails_ref[k : k + 1] << rel_bits)) << head_bits
        )
        codes[k * LANES : (k + 1) * LANES] = column(code)
    lane = iota((LANES, LANES), 1)
    for k in range(negs // LANES):
        ids = column(negs_ref[k : k + 1])
        for c in range(entities // LANES):
            hot_rows[k * LANES : (k + 1) * LANES, c * LANES : (c + 1) * LANES] = hot(
                ids == lane + c * LANES
            )
    neg_rows[...] = nn(hot_rows[:negs], entity_ref[...]).astype(BF16)

    pl.semaphore_wait(barrier, n_ent + 1)

    def exchange(src, dst, sems, step):
        target = lax.rem(me + step + 1, n_ent)
        return pltpu.make_async_remote_copy(
            src_ref=src.at[target],
            dst_ref=dst.at[me],
            send_sem=sems.at[0, target],
            recv_sem=sems.at[1, me],
            device_id=(target, rel),
            device_id_type=MESH,
        )

    def arrival(dst, sems, step):
        source = lax.rem(me + step + 1, n_ent)
        return pltpu.make_async_remote_copy(
            src_ref=dst.at[source],
            dst_ref=dst.at[source],
            send_sem=sems.at[0, source],
            recv_sem=sems.at[1, source],
            device_id=(source, rel),
            device_id_type=MESH,
        )

    def start_all(src, dst, sems):
        each(n_ent - 1, lambda step: exchange(src, dst, sems, step).start())

    def wait_all(dst, sems):
        each(n_ent - 1, lambda step: arrival(dst, sems, step).wait_recv())

    def drain_all(src, dst, sems):
        each(n_ent - 1, lambda step: exchange(src, dst, sems, step).wait_send())

    start_all(request_send, request_recv, request_sems)

    spread = hot(iota((block, width), 1) % block == iota((block, width), 0))
    spread_t = hot(iota((width, block), 0) % block == iota((width, block), 1))
    diagonal = iota((width, width), 0) // block == iota((width, width), 1) // block
    for r in range(r_count):
        rows = slice(r * width, (r + 1) * width)
        one = blocks_ref[rows]
        operators[rows] = jnp.where(diagonal, nn(one, spread), 0.0).astype(BF16)
        operators_t[rows] = jnp.where(diagonal, nt(spread_t, one), 0.0).astype(BF16)

    def rel_masks(rows):
        ids = (codes[rows] >> head_bits) & (r_count - 1)
        return [hot(ids == r) for r in range(r_count)]

    def mask_by_rel(source, masks, target, rows):
        for r in range(r_count):
            for c in range(width // LANES):
                at = r * width + c * LANES
                target[rows, at : at + LANES] = source[:, c * LANES : (c + 1) * LANES] * masks[r]

    wide_lane = iota((chunk, LANES), 1)

    def project(i):
        rows = slice(i * chunk, (i + 1) * chunk)
        ids = codes[rows] & (entities - 1)
        for c in range(entities // LANES):
            hot_rows[:, c * LANES : (c + 1) * LANES] = hot(ids == wide_lane + c * LANES)
        head = nn(hot_rows[...], entity_ref[...]).astype(BF16)
        mask_by_rel(head, rel_masks(rows), masked_heads, rows)
        proj = nn(masked_heads[rows], operators[...]).astype(BF16)
        projected[rows] = proj
        score = nt(proj, neg_rows[...])
        live = iota((chunk, negs), 0) + i * chunk < live_count
        weight = jnp.where(live, jax.nn.sigmoid(score) * (1.0 / negs), 0.0).astype(BF16)
        neg_weight[rows] = weight
        return tn(weight, proj)

    neg_grad = project(0)

    wait_all(request_recv, request_sems)
    request_rows = []
    lane8 = iota((8, LANES), 1) // slots
    for g in range(n_ent // per):
        row = request_recv[g * per]
        for q in range(1, per):
            row = jnp.where(lane8 == q, request_recv[g * per + q], row)
        row = row[:1]
        request_rows.append(row)
        ids = column(row)
        for c in range(entities // LANES):
            hot_rows[:LANES, c * LANES : (c + 1) * LANES] = hot(ids == lane + c * LANES)
        want_send[g * per : (g + 1) * per] = (
            nn(hot_rows[:LANES], entity_ref[...]).astype(BF16).reshape(per, slots, width)
        )
    fetched[me] = want_send[me]
    start_all(want_send, fetched, fetch_sems)

    for i in range(1, chunks):
        neg_grad = neg_grad + project(i)
    grads[neg_at : neg_at + negs] = neg_grad.astype(BF16)

    sub = iota((entities, LANES), 0)
    for k in range(edges // LANES):
        scatter_hot[:, k * LANES : (k + 1) * LANES] = hot(sub == heads_ref[k : k + 1])
    for k in range(negs // LANES):
        at = neg_at + k * LANES
        scatter_hot[:, at : at + LANES] = hot(sub == negs_ref[k : k + 1])
    for k, row in enumerate(request_rows):
        at = slot_at + k * LANES
        scatter_hot[:, at : at + LANES] = hot(sub == row)
    slot_sub = iota((slot_total, LANES), 0)
    for k in range(edges // LANES):
        tail_hot_t[:, k * LANES : (k + 1) * LANES] = hot(slot_sub == tails_ref[k : k + 1])

    wait_all(fetched, fetch_sems)
    table = fetched[...].reshape(slot_total, width)
    for i in range(chunks):
        rows = slice(i * chunk, (i + 1) * chunk)
        ids = codes[rows] >> (head_bits + rel_bits)
        tail_hot = jnp.concatenate(
            [hot(ids == wide_lane + c * LANES) for c in range(slot_total // LANES)], axis=1
        )
        tail = nn(tail_hot, table)
        proj = projected[rows].astype(F32)
        positive = jnp.sum(proj * tail, axis=1, keepdims=True)
        live = iota((chunk, 1), 0) + i * chunk < live_count
        pos_weight = jnp.where(live, -jax.nn.sigmoid(-positive), 0.0)
        weighted[rows] = (pos_weight * proj).astype(BF16)
        grad_proj[rows] = (pos_weight * tail + nn(neg_weight[rows], neg_rows[...])).astype(BF16)
    per_step = min(n_ent, 8)
    for g in range(n_ent // per_step):
        rows = slice(g * per_step * slots, (g + 1) * per_step * slots)
        slot_send[g * per_step : (g + 1) * per_step] = (
            nn(tail_hot_t[rows], weighted[...]).astype(BF16).reshape(per_step, slots, width)
        )
    slot_recv = grads.at[slot_at : slot_at + slot_total]

    def slot_copy(step):
        target = lax.rem(me + step + 1, n_ent)
        return pltpu.make_async_remote_copy(
            src_ref=slot_send.at[target],
            dst_ref=grads.at[pl.ds(pl.multiple_of(slot_at + me * slots, slots), slots)],
            send_sem=slot_sems.at[0, target],
            recv_sem=slot_sems.at[1, me],
            device_id=(target, rel),
            device_id_type=MESH,
        )

    def slot_arrival(step):
        source = lax.rem(me + step + 1, n_ent)
        return pltpu.make_async_remote_copy(
            src_ref=slot_send.at[source],
            dst_ref=grads.at[pl.ds(pl.multiple_of(slot_at + source * slots, slots), slots)],
            send_sem=slot_sems.at[0, source],
            recv_sem=slot_sems.at[1, source],
            device_id=(source, rel),
            device_id_type=MESH,
        )

    each(n_ent - 1, lambda step: slot_copy(step).start())
    grads[pl.ds(pl.multiple_of(slot_at + me * slots, slots), slots)] = slot_send[me]

    wire = rel_send.dtype
    per_owner = rel_send.shape[1]
    grad_proj_t[...] = jnp.transpose(grad_proj[...])
    block_of_lane = iota((block, width), 1) // block
    step_rows = min(block, per_owner)
    for r in range(r_count):
        outer = nn(grad_proj_t[...], masked_heads[:, r * width : (r + 1) * width])
        small = jnp.zeros((block, width), F32)
        for n in range(width // block):
            small = small + jnp.where(
                block_of_lane == n, outer[n * block : (n + 1) * block], 0.0
            )
        for c in range(width // LANES):
            for t in range(block // step_rows):
                flat = (r * (width // LANES) + c) * block + t * step_rows
                owner, at = flat // per_owner, flat % per_owner
                rel_send[owner, at : at + step_rows] = small[
                    t * step_rows : (t + 1) * step_rows, c * LANES : (c + 1) * LANES
                ].astype(wire)
    start_all(rel_send, rel_recv, rs_sems)
    rel_recv[me] = rel_send[me]

    for i in range(chunks):
        rows = slice(i * chunk, (i + 1) * chunk)
        mask_by_rel(grad_proj[rows], rel_masks(rows), masked_grads, slice(0, chunk))
        grads[rows] = nn(masked_grads[...], operators_t[...]).astype(BF16)

    each(n_ent - 1, lambda step: slot_arrival(step).wait_recv())

    pieces = half // chunk
    part_copies = []
    for q in range(pieces):
        at = pl.multiple_of((1 - core) * half + q * chunk, chunk)
        part_send[q] = nn(scatter_hot[pl.ds(at, chunk)], grads[...]).astype(BF16)
        copy = pltpu.make_async_remote_copy(
            src_ref=part_send.at[q],
            dst_ref=part_recv.at[q],
            send_sem=part_sems.at[0, q],
            recv_sem=part_sems.at[1, q],
            device_id=(me, near),
            device_id_type=MESH,
        )
        copy.start()
        part_copies.append(copy)
    cross_copies, near_copies = [], []
    for q in range(pieces):
        at = pl.multiple_of(core * half + q * chunk, chunk)
        own = nn(scatter_hot[pl.ds(at, chunk)], grads[...])
        part_copies[q].wait_recv()
        sum_a_ref[core, q] = (own + part_recv[q].astype(F32)).astype(BF16)
        copy = pltpu.make_async_remote_copy(
            src_ref=sum_a_ref.at[core, q],
            dst_ref=sum_b_ref.at[core, q],
            send_sem=cross_sems.at[0, q],
            recv_sem=cross_sems.at[1, q],
            device_id=(me, cross),
            device_id_type=MESH,
        )
        copy.start()
        cross_copies.append(copy)
        copy = pltpu.make_async_remote_copy(
            src_ref=sum_a_ref.at[core, q],
            dst_ref=sum_a_ref.at[core, q],
            send_sem=near_sems.at[0, q],
            recv_sem=near_sems.at[1, q],
            device_id=(me, near),
            device_id_type=MESH,
        )
        copy.start()
        near_copies.append(copy)

    far_copies = []

    def forward(q):
        cross_copies[q].wait_recv()
        copy = pltpu.make_async_remote_copy(
            src_ref=sum_b_ref.at[core, q],
            dst_ref=sum_b_ref.at[core, q],
            send_sem=far_sems.at[0, q],
            recv_sem=far_sems.at[1, q],
            device_id=(me, near),
            device_id_type=MESH,
        )
        copy.start()
        far_copies.append(copy)

    wait_all(rel_recv, rs_sems)
    total = rel_recv[0].astype(F32)
    for p in range(1, n_ent):
        total = total + rel_recv[p].astype(F32)
    rel_own[...] = total.astype(wire)
    rel_out_ref[me] = rel_own[...]

    def gather_copy(step):
        target = lax.rem(me + step + 1, n_ent)
        return pltpu.make_async_remote_copy(
            src_ref=rel_own,
            dst_ref=rel_out_ref.at[me],
            send_sem=ag_sems.at[0, target],
            recv_sem=ag_sems.at[1, me],
            device_id=(target, rel),
            device_id_type=MESH,
        )

    each(n_ent - 1, lambda step: gather_copy(step).start())
    for q in range(pieces):
        forward(q)

    wait_all(rel_out_ref, ag_sems)
    for copies in (near_copies, far_copies):
        for copy in copies:
            copy.wait_recv()
    drain_all(request_send, request_recv, request_sems)
    drain_all(want_send, fetched, fetch_sems)
    each(n_ent - 1, lambda step: slot_copy(step).wait_send())
    drain_all(rel_send, rel_recv, rs_sems)
    each(n_ent - 1, lambda step: gather_copy(step).wait_send())
    for copies in (part_copies, cross_copies, near_copies, far_copies):
        for copy in copies:
            copy.wait_send()


def finish(a_ref, b_ref, rel_ref, entity_ref, relation_ref):
    entity_ref[...] = a_ref[...].astype(F32) + b_ref[...].astype(F32)
    block = relation_ref.shape[1]
    for k in range(relation_ref.shape[0] // LANES):
        relation_ref[k * LANES : (k + 1) * LANES] = jnp.transpose(
            rel_ref[k * block : (k + 1) * block].astype(F32)
        )


def local(
    n_ent,
    n_rel,
    entity_rows,
    request_rows,
    edge_heads,
    edge_rels,
    edge_tails,
    edge_counts,
    negative_rows,
    relation_blocks,
):
    entities, width = entity_rows.shape
    slots = request_rows.shape[2]
    slot_total = n_ent * slots
    edges = edge_heads.shape[0]
    negs = negative_rows.shape[0]
    r_count, block_count, block, _ = relation_blocks.shape
    chunk = 256
    pieces = entities // 2 // chunk
    stacked = r_count * width
    flat_rows = stacked * block // LANES
    per_owner = flat_rows // n_ent
    wire = BF16 if per_owner % 16 == 0 else F32
    terms = edges + negs + slot_total
    vmem = pltpu.VMEM
    dma = pltpu.SemaphoreType.DMA
    spec = pl.BlockSpec(memory_space=pltpu.VMEM)
    out_shape = (
        jax.ShapeDtypeStruct((2, pieces, chunk, width), BF16),
        jax.ShapeDtypeStruct((2, pieces, chunk, width), BF16),
        jax.ShapeDtypeStruct((n_ent, per_owner, LANES), wire),
    )
    scratch = [
        vmem((n_ent, LANES), jnp.int32),
        vmem((n_ent, 8, LANES), jnp.int32),
        vmem((n_ent, 8, LANES), jnp.int32),
        vmem((n_ent, slots, width), BF16),
        vmem((n_ent, slots, width), BF16),
        vmem((n_ent, slots, width), BF16),
        vmem((entities, terms), BF16),
        vmem((terms, width), BF16),
        vmem((slot_total, edges), BF16),
        vmem((edges, LANES), jnp.int32),
        vmem((chunk, entities), BF16),
        vmem((stacked, width), BF16),
        vmem((stacked, width), BF16),
        vmem((edges, stacked), BF16),
        vmem((chunk, stacked), BF16),
        vmem((edges, width), BF16),
        vmem((edges, negs), BF16),
        vmem((negs, width), BF16),
        vmem((edges, width), BF16),
        vmem((edges, width), BF16),
        vmem((width, edges), BF16),
        vmem((pieces, chunk, width), BF16),
        vmem((pieces, chunk, width), BF16),
        vmem((n_ent, per_owner, LANES), wire),
        vmem((n_ent, per_owner, LANES), wire),
        vmem((per_owner, LANES), wire),
        dma((2, n_ent)),
        dma((2, n_ent)),
        dma((2, n_ent)),
        dma((2, pieces)),
        dma((2, pieces)),
        dma((2, pieces)),
        dma((2, pieces)),
        dma((2, n_ent)),
        dma((2, n_ent)),
    ]
    sum_a, sum_b, rel_flat = pl.pallas_call(
        functools.partial(kernel, (n_ent, n_rel)),
        out_shape=out_shape,
        in_specs=[pl.BlockSpec(memory_space=pltpu.SMEM)] + [spec] * 7,
        out_specs=(spec,) * 3,
        scratch_shapes=scratch,
        compiler_params=pltpu.CompilerParams(
            collective_id=0, has_side_effects=True, vmem_limit_bytes=36 * 1024 * 1024
        ),
    )(
        edge_counts,
        entity_rows,
        request_rows,
        edge_heads.reshape(edges // LANES, LANES),
        edge_rels.reshape(edges // LANES, LANES),
        edge_tails.reshape(edges // LANES, LANES),
        negative_rows.reshape(negs // LANES, LANES),
        relation_blocks.reshape(stacked, block),
    )
    steps = 4
    tiles = stacked // LANES // steps
    e_spec = pl.BlockSpec((entities // steps, width), lambda i: (i, 0))
    entity_grad, relation_grad = pl.pallas_call(
        finish,
        grid=(steps,),
        out_shape=(
            jax.ShapeDtypeStruct((entities, width), F32),
            jax.ShapeDtypeStruct((stacked, block), F32),
        ),
        in_specs=[e_spec, e_spec, pl.BlockSpec((tiles * block, LANES), lambda i: (i, 0))],
        out_specs=(e_spec, pl.BlockSpec((tiles * LANES, block), lambda i: (i, 0))),
    )(
        sum_a.reshape(entities, width),
        sum_b.reshape(entities, width),
        rel_flat.reshape(flat_rows, LANES),
    )
    return entity_grad, relation_grad.reshape(relation_blocks.shape)


def solution(mesh):
    in_specs = (
        P("ent", None),
        P("ent", None, None),
        P(("ent", "rel")),
        P(("ent", "rel")),
        P(("ent", "rel")),
        P(("ent", "rel")),
        P(("ent", "rel")),
        P("rel", None, None, None),
    )
    out_specs = (P("ent", None), P("rel", None, None, None))
    body = functools.partial(local, mesh.shape["ent"], mesh.shape["rel"])
    return jax.shard_map(body, mesh=mesh, in_specs=in_specs, out_specs=out_specs, check_vma=False)
```

```python
import functools

import jax
import jax.numpy as jnp
from jax import lax
from jax.experimental import pallas as pl
from jax.experimental.pallas import tpu as pltpu
from jax.sharding import PartitionSpec as P

MESH = pl.DeviceIdType.MESH
F32 = jnp.float32
BF16 = jnp.bfloat16
LANES = 128


def iota(shape, axis):
    return lax.broadcasted_iota(jnp.int32, shape, axis)


def hot(mask):
    return jnp.where(mask, 1.0, 0.0).astype(BF16)


def nn(a, b):
    return jnp.dot(a, b, preferred_element_type=F32)


def nt(a, b):
    return lax.dot_general(a, b, (((1,), (1,)), ((), ())), preferred_element_type=F32)


def tn(a, b):
    return lax.dot_general(a, b, (((0,), (0,)), ((), ())), preferred_element_type=F32)


def column(row):
    return jnp.transpose(jnp.broadcast_to(row, (LANES, LANES)))


def each(count, body):
    if count <= 8:
        for step in range(count):
            body(step)
    else:
        lax.fori_loop(0, count, lambda step, _: (body(step), 0)[1], 0)


def kernel(
    dims,
    counts_hbm,
    entity_hbm,
    request_hbm,
    heads_hbm,
    rels_hbm,
    tails_hbm,
    negs_hbm,
    blocks_hbm,
    entity_out,
    relation_out,
    counts_ref,
    entity_ref,
    request_ref,
    heads_ref,
    rels_ref,
    tails_ref,
    negs_ref,
    blocks_ref,
    sum_a_ref,
    sum_b_ref,
    rel_out_ref,
    entity_stage,
    relation_stage,
    request_wide,
    request_send,
    request_recv,
    want_send,
    fetched,
    slot_send,
    scatter_hot,
    grads,
    tail_hot_t,
    codes,
    hot_rows,
    operators,
    operators_t,
    masked_heads,
    masked_grads,
    projected,
    neg_weight,
    neg_rows,
    weighted,
    grad_proj,
    grad_proj_t,
    part_send,
    part_recv,
    rel_send,
    rel_recv,
    rel_own,
    request_sems,
    fetch_sems,
    slot_sems,
    part_sems,
    cross_sems,
    near_sems,
    far_sems,
    rs_sems,
    ag_sems,
    in_sems,
    entity_sems,
    relation_sems,
):
    n_ent, n_rel = dims
    me, rel = lax.axis_index("ent"), lax.axis_index("rel")
    core, side = rel % 2, rel // 2
    near = side * 2 + (1 - core)
    cross = (1 - side) * 2 + core
    entities, width = entity_ref.shape
    slots = request_ref.shape[2]
    slot_total = n_ent * slots
    edges = heads_ref.shape[0] * LANES
    negs = negs_ref.shape[0] * LANES
    block = blocks_ref.shape[1]
    r_count = blocks_ref.shape[0] // width
    chunk = masked_grads.shape[0]
    chunks = edges // chunk
    piece = sum_a_ref.shape[2]
    per = LANES // slots
    head_bits = (entities - 1).bit_length()
    rel_bits = (r_count - 1).bit_length()
    neg_at, slot_at = edges, edges + negs
    half = entities // 2

    loads = [
        pltpu.make_async_copy(src, dst, in_sems.at[k])
        for k, (src, dst) in enumerate(
            (
                (request_hbm, request_ref),
                (heads_hbm, heads_ref),
                (rels_hbm, rels_ref),
                (tails_hbm, tails_ref),
                (negs_hbm, negs_ref),
                (entity_hbm, entity_ref),
                (blocks_hbm, blocks_ref),
                (counts_hbm, counts_ref),
            )
        )
    ]
    for load in loads:
        load.start()

    barrier = pltpu.get_barrier_semaphore()

    def greet(step):
        pl.semaphore_signal(
            barrier, inc=1, device_id=(lax.rem(me + step + 1, n_ent), rel), device_id_type=MESH
        )

    each(n_ent - 1, greet)
    for partner in (near, cross):
        pl.semaphore_signal(barrier, inc=1, device_id=(me, partner), device_id_type=MESH)

    request_wide[...] = jnp.zeros_like(request_wide)
    loads[0].wait()
    request_wide[:, :slots] = request_ref[0]
    base = request_wide[...]
    wide = base
    for q in range(1, per):
        wide = wide + pltpu.roll(base, q * slots, 1)
    for p in range(n_ent):
        request_send[p] = jnp.broadcast_to(wide[p : p + 1], (8, LANES))
    request_recv[me] = request_send[me]

    for load in loads[1:5]:
        load.wait()
    for k in range(edges // LANES):
        code = heads_ref[k : k + 1] + (
            (rels_ref[k : k + 1] + (tails_ref[k : k + 1] << rel_bits)) << head_bits
        )
        codes[k * LANES : (k + 1) * LANES] = column(code)
    lane = iota((LANES, LANES), 1)
    for k in range(negs // LANES):
        ids = column(negs_ref[k : k + 1])
        for c in range(entities // LANES):
            hot_rows[k * LANES : (k + 1) * LANES, c * LANES : (c + 1) * LANES] = hot(
                ids == lane + c * LANES
            )
    loads[5].wait()
    neg_rows[...] = nn(hot_rows[:negs], entity_ref[...]).astype(BF16)

    pl.semaphore_wait(barrier, n_ent + 1)

    def exchange(src, dst, sems, step):
        target = lax.rem(me + step + 1, n_ent)
        return pltpu.make_async_remote_copy(
            src_ref=src.at[target],
            dst_ref=dst.at[me],
            send_sem=sems.at[0, target],
            recv_sem=sems.at[1, me],
            device_id=(target, rel),
            device_id_type=MESH,
        )

    def arrival(dst, sems, step):
        source = lax.rem(me + step + 1, n_ent)
        return pltpu.make_async_remote_copy(
            src_ref=dst.at[source],
            dst_ref=dst.at[source],
            send_sem=sems.at[0, source],
            recv_sem=sems.at[1, source],
            device_id=(source, rel),
            device_id_type=MESH,
        )

    def start_all(src, dst, sems):
        each(n_ent - 1, lambda step: exchange(src, dst, sems, step).start())

    def wait_all(dst, sems):
        each(n_ent - 1, lambda step: arrival(dst, sems, step).wait_recv())

    def drain_all(src, dst, sems):
        each(n_ent - 1, lambda step: exchange(src, dst, sems, step).wait_send())

    start_all(request_send, request_recv, request_sems)

    spread = hot(iota((block, width), 1) % block == iota((block, width), 0))
    spread_t = hot(iota((width, block), 0) % block == iota((width, block), 1))
    diagonal = iota((width, width), 0) // block == iota((width, width), 1) // block
    loads[6].wait()
    loads[7].wait()
    live_count = counts_ref[0]
    for r in range(r_count):
        rows = slice(r * width, (r + 1) * width)
        one = blocks_ref[rows]
        operators[rows] = jnp.where(diagonal, nn(one, spread), 0.0).astype(BF16)
        operators_t[rows] = jnp.where(diagonal, nt(spread_t, one), 0.0).astype(BF16)

    def rel_masks(rows):
        ids = (codes[rows] >> head_bits) & (r_count - 1)
        return [hot(ids == r) for r in range(r_count)]

    def mask_by_rel(source, masks, target, rows):
        for r in range(r_count):
            for c in range(width // LANES):
                at = r * width + c * LANES
                target[rows, at : at + LANES] = source[:, c * LANES : (c + 1) * LANES] * masks[r]

    wide_lane = iota((chunk, LANES), 1)

    def project(i):
        rows = slice(i * chunk, (i + 1) * chunk)
        ids = codes[rows] & (entities - 1)
        for c in range(entities // LANES):
            hot_rows[:, c * LANES : (c + 1) * LANES] = hot(ids == wide_lane + c * LANES)
        head = nn(hot_rows[...], entity_ref[...]).astype(BF16)
        mask_by_rel(head, rel_masks(rows), masked_heads, rows)
        proj = nn(masked_heads[rows], operators[...]).astype(BF16)
        projected[rows] = proj
        score = nt(proj, neg_rows[...])
        live = iota((chunk, negs), 0) + i * chunk < live_count
        weight = jnp.where(live, jax.nn.sigmoid(score) * (1.0 / negs), 0.0).astype(BF16)
        neg_weight[rows] = weight
        return tn(weight, proj)

    neg_grad = project(0)

    wait_all(request_recv, request_sems)
    request_rows = []
    lane8 = iota((8, LANES), 1) // slots
    for g in range(n_ent // per):
        row = request_recv[g * per]
        for q in range(1, per):
            row = jnp.where(lane8 == q, request_recv[g * per + q], row)
        row = row[:1]
        request_rows.append(row)
        ids = column(row)
        for c in range(entities // LANES):
            hot_rows[:LANES, c * LANES : (c + 1) * LANES] = hot(ids == lane + c * LANES)
        want_send[g * per : (g + 1) * per] = (
            nn(hot_rows[:LANES], entity_ref[...]).astype(BF16).reshape(per, slots, width)
        )
    fetched[me] = want_send[me]
    start_all(want_send, fetched, fetch_sems)

    for i in range(1, chunks):
        neg_grad = neg_grad + project(i)
    grads[neg_at : neg_at + negs] = neg_grad.astype(BF16)

    sub = iota((entities, LANES), 0)
    for k in range(edges // LANES):
        scatter_hot[:, k * LANES : (k + 1) * LANES] = hot(sub == heads_ref[k : k + 1])
    for k in range(negs // LANES):
        at = neg_at + k * LANES
        scatter_hot[:, at : at + LANES] = hot(sub == negs_ref[k : k + 1])
    for k, row in enumerate(request_rows):
        at = slot_at + k * LANES
        scatter_hot[:, at : at + LANES] = hot(sub == row)
    slot_sub = iota((slot_total, LANES), 0)
    for k in range(edges // LANES):
        tail_hot_t[:, k * LANES : (k + 1) * LANES] = hot(slot_sub == tails_ref[k : k + 1])

    wait_all(fetched, fetch_sems)
    table = fetched[...].reshape(slot_total, width)
    for i in range(chunks):
        rows = slice(i * chunk, (i + 1) * chunk)
        ids = codes[rows] >> (head_bits + rel_bits)
        tail_hot = jnp.concatenate(
            [hot(ids == wide_lane + c * LANES) for c in range(slot_total // LANES)], axis=1
        )
        tail = nn(tail_hot, table)
        proj = projected[rows].astype(F32)
        positive = jnp.sum(proj * tail, axis=1, keepdims=True)
        live = iota((chunk, 1), 0) + i * chunk < live_count
        pos_weight = jnp.where(live, -jax.nn.sigmoid(-positive), 0.0)
        weighted[rows] = (pos_weight * proj).astype(BF16)
        grad_proj[rows] = (pos_weight * tail + nn(neg_weight[rows], neg_rows[...])).astype(BF16)
    per_step = min(n_ent, 8)
    for g in range(n_ent // per_step):
        rows = slice(g * per_step * slots, (g + 1) * per_step * slots)
        slot_send[g * per_step : (g + 1) * per_step] = (
            nn(tail_hot_t[rows], weighted[...]).astype(BF16).reshape(per_step, slots, width)
        )
    slot_recv = grads.at[slot_at : slot_at + slot_total]

    def slot_copy(step):
        target = lax.rem(me + step + 1, n_ent)
        return pltpu.make_async_remote_copy(
            src_ref=slot_send.at[target],
            dst_ref=grads.at[pl.ds(pl.multiple_of(slot_at + me * slots, slots), slots)],
            send_sem=slot_sems.at[0, target],
            recv_sem=slot_sems.at[1, me],
            device_id=(target, rel),
            device_id_type=MESH,
        )

    def slot_arrival(step):
        source = lax.rem(me + step + 1, n_ent)
        return pltpu.make_async_remote_copy(
            src_ref=slot_send.at[source],
            dst_ref=grads.at[pl.ds(pl.multiple_of(slot_at + source * slots, slots), slots)],
            send_sem=slot_sems.at[0, source],
            recv_sem=slot_sems.at[1, source],
            device_id=(source, rel),
            device_id_type=MESH,
        )

    each(n_ent - 1, lambda step: slot_copy(step).start())
    grads[pl.ds(pl.multiple_of(slot_at + me * slots, slots), slots)] = slot_send[me]

    wire = rel_send.dtype
    per_owner = rel_send.shape[1]
    grad_proj_t[...] = jnp.transpose(grad_proj[...])
    block_of_lane = iota((block, width), 1) // block
    step_rows = min(block, per_owner)
    for r in range(r_count):
        outer = nn(grad_proj_t[...], masked_heads[:, r * width : (r + 1) * width])
        small = jnp.zeros((block, width), F32)
        for n in range(width // block):
            small = small + jnp.where(
                block_of_lane == n, outer[n * block : (n + 1) * block], 0.0
            )
        for c in range(width // LANES):
            for t in range(block // step_rows):
                flat = (r * (width // LANES) + c) * block + t * step_rows
                owner, at = flat // per_owner, flat % per_owner
                rel_send[owner, at : at + step_rows] = small[
                    t * step_rows : (t + 1) * step_rows, c * LANES : (c + 1) * LANES
                ].astype(wire)
    start_all(rel_send, rel_recv, rs_sems)
    rel_recv[me] = rel_send[me]

    for i in range(chunks):
        rows = slice(i * chunk, (i + 1) * chunk)
        mask_by_rel(grad_proj[rows], rel_masks(rows), masked_grads, slice(0, chunk))
        grads[rows] = nn(masked_grads[...], operators_t[...]).astype(BF16)

    each(n_ent - 1, lambda step: slot_arrival(step).wait_recv())

    pieces = half // piece
    pair = 2
    part_copies, cross_copies, near_copies, far_copies = [], [], [], []

    def near_copy(src, dst, sems, q, target):
        copy = pltpu.make_async_remote_copy(
            src_ref=src,
            dst_ref=dst,
            send_sem=sems.at[0, q],
            recv_sem=sems.at[1, q],
            device_id=(me, target),
            device_id_type=MESH,
        )
        copy.start()
        return copy

    for g in range(pieces // pair):
        at = pl.multiple_of((1 - core) * half + g * pair * piece, pair * piece)
        part = nn(scatter_hot[pl.ds(at, pair * piece)], grads[...]).astype(BF16)
        for q in range(g * pair, (g + 1) * pair):
            low = (q - g * pair) * piece
            part_send[q] = part[low : low + piece]
            part_copies.append(near_copy(part_send.at[q], part_recv.at[q], part_sems, q, near))
    for g in range(pieces // pair):
        at = pl.multiple_of(core * half + g * pair * piece, pair * piece)
        own = nn(scatter_hot[pl.ds(at, pair * piece)], grads[...])
        for q in range(g * pair, (g + 1) * pair):
            low = (q - g * pair) * piece
            part_copies[q].wait_recv()
            sum_a_ref[core, q] = (own[low : low + piece] + part_recv[q].astype(F32)).astype(BF16)
            mine = sum_a_ref.at[core, q]
            cross_copies.append(near_copy(mine, sum_b_ref.at[core, q], cross_sems, q, cross))
            near_copies.append(near_copy(mine, mine, near_sems, q, near))

    def write_entity(which, q):
        entity_stage[which, q] = sum_a_ref[which, q].astype(F32) + sum_b_ref[which, q].astype(F32)
        copy = pltpu.make_async_copy(
            entity_stage.at[which, q], entity_out.at[which, q], entity_sems.at[which, q]
        )
        copy.start()
        return copy

    wait_all(rel_recv, rs_sems)
    total = rel_recv[0].astype(F32)
    for p in range(1, n_ent):
        total = total + rel_recv[p].astype(F32)
    rel_own[...] = total.astype(wire)
    rel_out_ref[me] = rel_own[...]

    def gather_copy(step):
        target = lax.rem(me + step + 1, n_ent)
        return pltpu.make_async_remote_copy(
            src_ref=rel_own,
            dst_ref=rel_out_ref.at[me],
            send_sem=ag_sems.at[0, target],
            recv_sem=ag_sems.at[1, me],
            device_id=(target, rel),
            device_id_type=MESH,
        )

    each(n_ent - 1, lambda step: gather_copy(step).start())
    stores = []

    def forward(q):
        cross_copies[q].wait_recv()
        theirs = sum_b_ref.at[core, q]
        far_copies.append(near_copy(theirs, theirs, far_sems, q, near))
        stores.append(write_entity(core, q))

    def finish_other(q):
        near_copies[q].wait_recv()
        far_copies[q].wait_recv()
        stores.append(write_entity(1 - core, q))

    for q in range(pieces - 1):
        forward(q)
    wait_all(rel_out_ref, ag_sems)
    for k in range(relation_stage.shape[0] // LANES):
        parts = []
        for t in range(block // step_rows):
            owner, at = divmod(k * block + t * step_rows, per_owner)
            parts.append(rel_out_ref[owner, at : at + step_rows].astype(F32))
        tile = parts[0] if len(parts) == 1 else jnp.concatenate(parts, axis=0)
        relation_stage[k * LANES : (k + 1) * LANES] = jnp.transpose(tile)
    store_rows = relation_stage.shape[0] // relation_sems.shape[0]
    for k in range(relation_sems.shape[0]):
        rows = pl.ds(k * store_rows, store_rows)
        copy = pltpu.make_async_copy(
            relation_stage.at[rows], relation_out.at[rows], relation_sems.at[k]
        )
        copy.start()
        stores.append(copy)
    for q in range(pieces - 1):
        finish_other(q)
    forward(pieces - 1)
    finish_other(pieces - 1)
    for copy in stores:
        copy.wait()
    drain_all(request_send, request_recv, request_sems)
    drain_all(want_send, fetched, fetch_sems)
    each(n_ent - 1, lambda step: slot_copy(step).wait_send())
    drain_all(rel_send, rel_recv, rs_sems)
    each(n_ent - 1, lambda step: gather_copy(step).wait_send())
    for copies in (part_copies, cross_copies, near_copies, far_copies):
        for copy in copies:
            copy.wait_send()


def finish(entity_ref, relation_ref, entity_out, relation_out, sems):
    copies = []
    count = sems.shape[1]
    for k, (src, dst) in enumerate(((relation_ref, relation_out), (entity_ref, entity_out))):
        rows = src.shape[0] // count
        for c in range(count):
            at = pl.ds(c * rows, rows)
            copies.append(pltpu.make_async_copy(src.at[at], dst.at[at], sems.at[k, c]))
    for copy in copies:
        copy.start()
    for copy in copies:
        copy.wait()


def local(
    n_ent,
    n_rel,
    entity_rows,
    request_rows,
    edge_heads,
    edge_rels,
    edge_tails,
    edge_counts,
    negative_rows,
    relation_blocks,
):
    entities, width = entity_rows.shape
    slots = request_rows.shape[2]
    slot_total = n_ent * slots
    edges = edge_heads.shape[0]
    negs = negative_rows.shape[0]
    r_count, block_count, block, _ = relation_blocks.shape
    chunk = min(512, edges)
    piece = 128
    pieces = entities // 2 // piece
    stacked = r_count * width
    flat_rows = stacked * block // LANES
    per_owner = flat_rows // n_ent
    wire = BF16 if per_owner % 16 == 0 else F32
    terms = edges + negs + slot_total
    vmem = pltpu.VMEM
    dma = pltpu.SemaphoreType.DMA
    spec = pl.BlockSpec(memory_space=pl.ANY)
    out_shape = (
        jax.ShapeDtypeStruct((2, pieces, piece, width), F32),
        jax.ShapeDtypeStruct((stacked, block), F32),
    )
    scratch = [
        pltpu.SMEM((1,), jnp.int32),
        vmem((entities, width), BF16),
        vmem(request_rows.shape, jnp.int32),
        vmem((edges // LANES, LANES), jnp.int32),
        vmem((edges // LANES, LANES), jnp.int32),
        vmem((edges // LANES, LANES), jnp.int32),
        vmem((negs // LANES, LANES), jnp.int32),
        vmem((stacked, block), BF16),
        vmem((2, pieces, piece, width), BF16),
        vmem((2, pieces, piece, width), BF16),
        vmem((n_ent, per_owner, LANES), wire),
        vmem((2, pieces, piece, width), F32),
        vmem((stacked, block), F32),
        vmem((n_ent, LANES), jnp.int32),
        vmem((n_ent, 8, LANES), jnp.int32),
        vmem((n_ent, 8, LANES), jnp.int32),
        vmem((n_ent, slots, width), BF16),
        vmem((n_ent, slots, width), BF16),
        vmem((n_ent, slots, width), BF16),
        vmem((entities, terms), BF16),
        vmem((terms, width), BF16),
        vmem((slot_total, edges), BF16),
        vmem((edges, LANES), jnp.int32),
        vmem((chunk, entities), BF16),
        vmem((stacked, width), BF16),
        vmem((stacked, width), BF16),
        vmem((edges, stacked), BF16),
        vmem((chunk, stacked), BF16),
        vmem((edges, width), BF16),
        vmem((edges, negs), BF16),
        vmem((negs, width), BF16),
        vmem((edges, width), BF16),
        vmem((edges, width), BF16),
        vmem((width, edges), BF16),
        vmem((pieces, piece, width), BF16),
        vmem((pieces, piece, width), BF16),
        vmem((n_ent, per_owner, LANES), wire),
        vmem((n_ent, per_owner, LANES), wire),
        vmem((per_owner, LANES), wire),
        dma((2, n_ent)),
        dma((2, n_ent)),
        dma((2, n_ent)),
        dma((2, pieces)),
        dma((2, pieces)),
        dma((2, pieces)),
        dma((2, pieces)),
        dma((2, n_ent)),
        dma((2, n_ent)),
        dma((8,)),
        dma((2, pieces)),
        dma((4,)),
    ]
    entity_sum, relation_sum = pl.pallas_call(
        functools.partial(kernel, (n_ent, n_rel)),
        out_shape=out_shape,
        in_specs=[spec] * 8,
        out_specs=(spec,) * 2,
        scratch_shapes=scratch,
        compiler_params=pltpu.CompilerParams(
            collective_id=0, has_side_effects=True, vmem_limit_bytes=56 * 1024 * 1024
        ),
    )(
        edge_counts,
        entity_rows,
        request_rows,
        edge_heads.reshape(edges // LANES, LANES),
        edge_rels.reshape(edges // LANES, LANES),
        edge_tails.reshape(edges // LANES, LANES),
        negative_rows.reshape(negs // LANES, LANES),
        relation_blocks.reshape(stacked, block),
    )
    entity_grad, relation_grad = pl.pallas_call(
        finish,
        out_shape=(
            jax.ShapeDtypeStruct((entities, width), F32),
            jax.ShapeDtypeStruct((stacked, block), F32),
        ),
        in_specs=[spec] * 2,
        out_specs=(spec,) * 2,
        scratch_shapes=[dma((2, 8))],
        compiler_params=pltpu.CompilerParams(vmem_limit_bytes=56 * 1024 * 1024),
    )(entity_sum.reshape(entities, width), relation_sum)
    return entity_grad, relation_grad.reshape(relation_blocks.shape)


def solution(mesh):
    in_specs = (
        P("ent", None),
        P("ent", None, None),
        P(("ent", "rel")),
        P(("ent", "rel")),
        P(("ent", "rel")),
        P(("ent", "rel")),
        P(("ent", "rel")),
        P("rel", None, None, None),
    )
    out_specs = (P("ent", None), P("rel", None, None, None))
    body = functools.partial(local, mesh.shape["ent"], mesh.shape["rel"])
    return jax.shard_map(body, mesh=mesh, in_specs=in_specs, out_specs=out_specs, check_vma=False)
```

```python
import functools

import jax
import jax.numpy as jnp
from jax import lax
from jax.experimental import pallas as pl
from jax.experimental.pallas import tpu as pltpu
from jax.sharding import PartitionSpec as P

MESH = pl.DeviceIdType.MESH
F32 = jnp.float32
BF16 = jnp.bfloat16
LANES = 128


def iota(shape, axis):
    return lax.broadcasted_iota(jnp.int32, shape, axis)


def hot(mask):
    return jnp.where(mask, 1.0, 0.0).astype(BF16)


def nn(a, b):
    return jnp.dot(a, b, preferred_element_type=F32)


def nt(a, b):
    return lax.dot_general(a, b, (((1,), (1,)), ((), ())), preferred_element_type=F32)


def tn(a, b):
    return lax.dot_general(a, b, (((0,), (0,)), ((), ())), preferred_element_type=F32)


def column(row):
    return jnp.transpose(jnp.broadcast_to(row, (LANES, LANES)))


def each(count, body):
    if count <= 8:
        for step in range(count):
            body(step)
    else:
        lax.fori_loop(0, count, lambda step, _: (body(step), 0)[1], 0)


def kernel(
    dims,
    counts_hbm,
    entity_hbm,
    request_hbm,
    heads_hbm,
    rels_hbm,
    tails_hbm,
    negs_hbm,
    blocks_hbm,
    entity_out,
    relation_out,
    counts_ref,
    entity_ref,
    request_ref,
    heads_ref,
    rels_ref,
    tails_ref,
    negs_ref,
    blocks_ref,
    sum_a_ref,
    sum_b_ref,
    rel_out_ref,
    entity_stage,
    request_wide,
    request_send,
    request_recv,
    want_send,
    fetched,
    slot_send,
    scatter_hot,
    grads,
    tail_hot_t,
    codes,
    hot_rows,
    operators,
    operators_t,
    masked_heads,
    masked_grads,
    projected,
    neg_weight,
    neg_rows,
    weighted,
    grad_proj,
    grad_proj_t,
    part_send,
    part_recv,
    rel_send,
    rel_recv,
    rel_own,
    request_sems,
    fetch_sems,
    slot_sems,
    part_sems,
    cross_sems,
    near_sems,
    far_sems,
    rs_sems,
    ag_sems,
    in_sems,
    entity_sems,
    relation_sems,
):
    n_ent, n_rel = dims
    me, rel = lax.axis_index("ent"), lax.axis_index("rel")
    core, side = rel % 2, rel // 2
    near = side * 2 + (1 - core)
    cross = (1 - side) * 2 + core
    entities, width = entity_ref.shape
    slots = request_ref.shape[2]
    slot_total = n_ent * slots
    edges = heads_ref.shape[0] * LANES
    negs = negs_ref.shape[0] * LANES
    block = blocks_ref.shape[1]
    r_count = blocks_ref.shape[0] // width
    chunk = masked_grads.shape[0]
    chunks = edges // chunk
    piece = sum_a_ref.shape[2]
    per = LANES // slots
    head_bits = (entities - 1).bit_length()
    rel_bits = (r_count - 1).bit_length()
    neg_at, slot_at = edges, edges + negs
    half = entities // 2

    loads = [
        pltpu.make_async_copy(src, dst, in_sems.at[k])
        for k, (src, dst) in enumerate(
            (
                (request_hbm, request_ref),
                (heads_hbm, heads_ref),
                (rels_hbm, rels_ref),
                (tails_hbm, tails_ref),
                (negs_hbm, negs_ref),
                (entity_hbm, entity_ref),
                (blocks_hbm, blocks_ref),
                (counts_hbm, counts_ref),
            )
        )
    ]
    for load in loads:
        load.start()

    barrier = pltpu.get_barrier_semaphore()

    def greet(step):
        pl.semaphore_signal(
            barrier, inc=1, device_id=(lax.rem(me + step + 1, n_ent), rel), device_id_type=MESH
        )

    each(n_ent - 1, greet)
    for partner in (near, cross):
        pl.semaphore_signal(barrier, inc=1, device_id=(me, partner), device_id_type=MESH)

    request_wide[...] = jnp.zeros_like(request_wide)
    loads[0].wait()
    request_wide[:, :slots] = request_ref[0]
    base = request_wide[...]
    wide = base
    for q in range(1, per):
        wide = wide + pltpu.roll(base, q * slots, 1)
    for p in range(n_ent):
        request_send[p] = jnp.broadcast_to(wide[p : p + 1], (8, LANES))
    request_recv[me] = request_send[me]

    for load in loads[1:5]:
        load.wait()
    for k in range(edges // LANES):
        code = heads_ref[k : k + 1] + (
            (rels_ref[k : k + 1] + (tails_ref[k : k + 1] << rel_bits)) << head_bits
        )
        codes[k * LANES : (k + 1) * LANES] = column(code)
    lane = iota((LANES, LANES), 1)
    for k in range(negs // LANES):
        ids = column(negs_ref[k : k + 1])
        for c in range(entities // LANES):
            hot_rows[k * LANES : (k + 1) * LANES, c * LANES : (c + 1) * LANES] = hot(
                ids == lane + c * LANES
            )
    loads[5].wait()
    neg_rows[...] = nn(hot_rows[:negs], entity_ref[...]).astype(BF16)

    pl.semaphore_wait(barrier, n_ent + 1)

    def exchange(src, dst, sems, step):
        target = lax.rem(me + step + 1, n_ent)
        return pltpu.make_async_remote_copy(
            src_ref=src.at[target],
            dst_ref=dst.at[me],
            send_sem=sems.at[0, target],
            recv_sem=sems.at[1, me],
            device_id=(target, rel),
            device_id_type=MESH,
        )

    def arrival(dst, sems, step):
        source = lax.rem(me + step + 1, n_ent)
        return pltpu.make_async_remote_copy(
            src_ref=dst.at[source],
            dst_ref=dst.at[source],
            send_sem=sems.at[0, source],
            recv_sem=sems.at[1, source],
            device_id=(source, rel),
            device_id_type=MESH,
        )

    def start_all(src, dst, sems):
        each(n_ent - 1, lambda step: exchange(src, dst, sems, step).start())

    def wait_all(dst, sems):
        each(n_ent - 1, lambda step: arrival(dst, sems, step).wait_recv())

    def drain_all(src, dst, sems):
        each(n_ent - 1, lambda step: exchange(src, dst, sems, step).wait_send())

    start_all(request_send, request_recv, request_sems)

    spread = hot(iota((block, width), 1) % block == iota((block, width), 0))
    spread_t = hot(iota((width, block), 0) % block == iota((width, block), 1))
    diagonal = iota((width, width), 0) // block == iota((width, width), 1) // block
    loads[6].wait()
    loads[7].wait()
    live_count = counts_ref[0]
    for r in range(r_count):
        rows = slice(r * width, (r + 1) * width)
        one = blocks_ref[rows]
        operators[rows] = jnp.where(diagonal, nn(one, spread), 0.0).astype(BF16)
        operators_t[rows] = jnp.where(diagonal, nt(spread_t, one), 0.0).astype(BF16)

    def rel_masks(rows):
        ids = (codes[rows] >> head_bits) & (r_count - 1)
        return [hot(ids == r) for r in range(r_count)]

    def mask_by_rel(source, masks, target, rows):
        for r in range(r_count):
            for c in range(width // LANES):
                at = r * width + c * LANES
                target[rows, at : at + LANES] = source[:, c * LANES : (c + 1) * LANES] * masks[r]

    wide_lane = iota((chunk, LANES), 1)

    def project(i):
        rows = slice(i * chunk, (i + 1) * chunk)
        ids = codes[rows] & (entities - 1)
        for c in range(entities // LANES):
            hot_rows[:, c * LANES : (c + 1) * LANES] = hot(ids == wide_lane + c * LANES)
        head = nn(hot_rows[...], entity_ref[...]).astype(BF16)
        mask_by_rel(head, rel_masks(rows), masked_heads, rows)
        proj = nn(masked_heads[rows], operators[...]).astype(BF16)
        projected[rows] = proj
        score = nt(proj, neg_rows[...])
        live = iota((chunk, negs), 0) + i * chunk < live_count
        weight = jnp.where(live, jax.nn.sigmoid(score) * (1.0 / negs), 0.0).astype(BF16)
        neg_weight[rows] = weight
        return tn(weight, proj)

    neg_grad = project(0)

    wait_all(request_recv, request_sems)
    request_rows = []
    lane8 = iota((8, LANES), 1) // slots
    for g in range(n_ent // per):
        row = request_recv[g * per]
        for q in range(1, per):
            row = jnp.where(lane8 == q, request_recv[g * per + q], row)
        row = row[:1]
        request_rows.append(row)
        ids = column(row)
        for c in range(entities // LANES):
            hot_rows[:LANES, c * LANES : (c + 1) * LANES] = hot(ids == lane + c * LANES)
        want_send[g * per : (g + 1) * per] = (
            nn(hot_rows[:LANES], entity_ref[...]).astype(BF16).reshape(per, slots, width)
        )
    fetched[me] = want_send[me]
    start_all(want_send, fetched, fetch_sems)

    for i in range(1, chunks):
        neg_grad = neg_grad + project(i)
    grads[neg_at : neg_at + negs] = neg_grad.astype(BF16)

    sub = iota((entities, LANES), 0)
    for k in range(edges // LANES):
        scatter_hot[:, k * LANES : (k + 1) * LANES] = hot(sub == heads_ref[k : k + 1])
    for k in range(negs // LANES):
        at = neg_at + k * LANES
        scatter_hot[:, at : at + LANES] = hot(sub == negs_ref[k : k + 1])
    for k, row in enumerate(request_rows):
        at = slot_at + k * LANES
        scatter_hot[:, at : at + LANES] = hot(sub == row)
    slot_sub = iota((slot_total, LANES), 0)
    for k in range(edges // LANES):
        tail_hot_t[:, k * LANES : (k + 1) * LANES] = hot(slot_sub == tails_ref[k : k + 1])

    wait_all(fetched, fetch_sems)
    table = fetched[...].reshape(slot_total, width)
    for i in range(chunks):
        rows = slice(i * chunk, (i + 1) * chunk)
        ids = codes[rows] >> (head_bits + rel_bits)
        tail_hot = jnp.concatenate(
            [hot(ids == wide_lane + c * LANES) for c in range(slot_total // LANES)], axis=1
        )
        tail = nn(tail_hot, table)
        proj = projected[rows].astype(F32)
        positive = jnp.sum(proj * tail, axis=1, keepdims=True)
        live = iota((chunk, 1), 0) + i * chunk < live_count
        pos_weight = jnp.where(live, -jax.nn.sigmoid(-positive), 0.0)
        weighted[rows] = (pos_weight * proj).astype(BF16)
        grad_proj[rows] = (pos_weight * tail + nn(neg_weight[rows], neg_rows[...])).astype(BF16)
    per_step = min(n_ent, 8)
    for g in range(n_ent // per_step):
        rows = slice(g * per_step * slots, (g + 1) * per_step * slots)
        slot_send[g * per_step : (g + 1) * per_step] = (
            nn(tail_hot_t[rows], weighted[...]).astype(BF16).reshape(per_step, slots, width)
        )
    slot_recv = grads.at[slot_at : slot_at + slot_total]

    def slot_copy(step):
        target = lax.rem(me + step + 1, n_ent)
        return pltpu.make_async_remote_copy(
            src_ref=slot_send.at[target],
            dst_ref=grads.at[pl.ds(pl.multiple_of(slot_at + me * slots, slots), slots)],
            send_sem=slot_sems.at[0, target],
            recv_sem=slot_sems.at[1, me],
            device_id=(target, rel),
            device_id_type=MESH,
        )

    def slot_arrival(step):
        source = lax.rem(me + step + 1, n_ent)
        return pltpu.make_async_remote_copy(
            src_ref=slot_send.at[source],
            dst_ref=grads.at[pl.ds(pl.multiple_of(slot_at + source * slots, slots), slots)],
            send_sem=slot_sems.at[0, source],
            recv_sem=slot_sems.at[1, source],
            device_id=(source, rel),
            device_id_type=MESH,
        )

    each(n_ent - 1, lambda step: slot_copy(step).start())
    grads[pl.ds(pl.multiple_of(slot_at + me * slots, slots), slots)] = slot_send[me]

    wire = rel_send.dtype
    per_owner = rel_send.shape[1]
    grad_proj_t[...] = jnp.transpose(grad_proj[...])
    block_of_lane = iota((block, width), 1) // block
    step_rows = min(block, per_owner)
    owners_per_r = n_ent // r_count

    def relation_terms(first, last):
        for r in range(first, last):
            outer = nn(grad_proj_t[...], masked_heads[:, r * width : (r + 1) * width])
            small = jnp.zeros((block, width), F32)
            for n in range(width // block):
                small = small + jnp.where(
                    block_of_lane == n, outer[n * block : (n + 1) * block], 0.0
                )
            for c in range(width // LANES):
                for t in range(block // step_rows):
                    flat = (r * (width // LANES) + c) * block + t * step_rows
                    owner, at = flat // per_owner, flat % per_owner
                    rel_send[owner, at : at + step_rows] = small[
                        t * step_rows : (t + 1) * step_rows, c * LANES : (c + 1) * LANES
                    ].astype(wire)
            for owner in range(r * owners_per_r, (r + 1) * owners_per_r):

                @pl.when(owner != me)
                def _():
                    pltpu.make_async_remote_copy(
                        src_ref=rel_send.at[owner],
                        dst_ref=rel_recv.at[me],
                        send_sem=rs_sems.at[0, owner],
                        recv_sem=rs_sems.at[1, me],
                        device_id=(owner, rel),
                        device_id_type=MESH,
                    ).start()

    relation_terms(0, r_count // 2)

    for i in range(chunks):
        rows = slice(i * chunk, (i + 1) * chunk)
        mask_by_rel(grad_proj[rows], rel_masks(rows), masked_grads, slice(0, chunk))
        grads[rows] = nn(masked_grads[...], operators_t[...]).astype(BF16)

    each(n_ent - 1, lambda step: slot_arrival(step).wait_recv())

    pieces = half // piece
    pair = 2
    part_copies, cross_copies, near_copies, far_copies = [], [], [], []

    def near_copy(src, dst, sems, q, target):
        copy = pltpu.make_async_remote_copy(
            src_ref=src,
            dst_ref=dst,
            send_sem=sems.at[0, q],
            recv_sem=sems.at[1, q],
            device_id=(me, target),
            device_id_type=MESH,
        )
        copy.start()
        return copy

    for g in range(pieces // pair):
        at = pl.multiple_of((1 - core) * half + g * pair * piece, pair * piece)
        part = nn(scatter_hot[pl.ds(at, pair * piece)], grads[...]).astype(BF16)
        for q in range(g * pair, (g + 1) * pair):
            low = (q - g * pair) * piece
            part_send[q] = part[low : low + piece]
            part_copies.append(near_copy(part_send.at[q], part_recv.at[q], part_sems, q, near))
    for g in range(pieces // pair):
        at = pl.multiple_of(core * half + g * pair * piece, pair * piece)
        own = nn(scatter_hot[pl.ds(at, pair * piece)], grads[...])
        for q in range(g * pair, (g + 1) * pair):
            low = (q - g * pair) * piece
            part_copies[q].wait_recv()
            sum_a_ref[core, q] = (own[low : low + piece] + part_recv[q].astype(F32)).astype(BF16)
            mine = sum_a_ref.at[core, q]
            cross_copies.append(near_copy(mine, sum_b_ref.at[core, q], cross_sems, q, cross))
            near_copies.append(near_copy(mine, mine, near_sems, q, near))

    def write_entity(which, q):
        entity_stage[which, q] = sum_a_ref[which, q].astype(F32) + sum_b_ref[which, q].astype(F32)
        copy = pltpu.make_async_copy(
            entity_stage.at[which, q], entity_out.at[which, q], entity_sems.at[which, q]
        )
        copy.start()
        return copy

    relation_terms(r_count // 2, r_count)
    rel_recv[me] = rel_send[me]
    wait_all(rel_recv, rs_sems)
    total = rel_recv[0].astype(F32)
    for p in range(1, n_ent):
        total = total + rel_recv[p].astype(F32)
    rel_own[...] = total.astype(wire)
    rel_out_ref[me] = rel_own[...]

    def gather_copy(step):
        target = lax.rem(me + step + 1, n_ent)
        return pltpu.make_async_remote_copy(
            src_ref=rel_own,
            dst_ref=rel_out_ref.at[me],
            send_sem=ag_sems.at[0, target],
            recv_sem=ag_sems.at[1, me],
            device_id=(target, rel),
            device_id_type=MESH,
        )

    each(n_ent - 1, lambda step: gather_copy(step).start())
    stores = []

    def forward(q):
        cross_copies[q].wait_recv()
        theirs = sum_b_ref.at[core, q]
        far_copies.append(near_copy(theirs, theirs, far_sems, q, near))
        stores.append(write_entity(core, q))

    def finish_other(q):
        near_copies[q].wait_recv()
        far_copies[q].wait_recv()
        stores.append(write_entity(1 - core, q))

    for q in range(pieces - 1):
        forward(q)
    wait_all(rel_out_ref, ag_sems)
    copy = pltpu.make_async_copy(rel_out_ref, relation_out, relation_sems.at[0])
    copy.start()
    stores.append(copy)
    for q in range(pieces - 1):
        finish_other(q)
    forward(pieces - 1)
    finish_other(pieces - 1)
    for copy in stores:
        copy.wait()
    drain_all(request_send, request_recv, request_sems)
    drain_all(want_send, fetched, fetch_sems)
    each(n_ent - 1, lambda step: slot_copy(step).wait_send())
    drain_all(rel_send, rel_recv, rs_sems)
    each(n_ent - 1, lambda step: gather_copy(step).wait_send())
    for copies in (part_copies, cross_copies, near_copies, far_copies):
        for copy in copies:
            copy.wait_send()


def finish(
    entity_ref, relation_ref, entity_out, relation_out, rel_in, rel_stage, stage, in_sems, out_sems
):
    count = out_sems.shape[1]
    rows = stage.shape[0] // count
    tall = rel_stage.shape[0] // count
    block = rel_stage.shape[1]
    rel_load = pltpu.make_async_copy(relation_ref, rel_in, in_sems.at[count])
    rel_load.start()
    loads, stores = [], []
    for c in range(count):
        at = pl.ds(c * rows, rows)
        loads.append(pltpu.make_async_copy(entity_ref.at[at], stage.at[at], in_sems.at[c]))
        loads[c].start()
    rel_load.wait()
    for c in range(count):
        for k in range(c * tall // LANES, (c + 1) * tall // LANES):
            rel_stage[k * LANES : (k + 1) * LANES] = jnp.transpose(
                rel_in[k * block : (k + 1) * block].astype(F32)
            )
        at = pl.ds(c * tall, tall)
        stores.append(
            pltpu.make_async_copy(rel_stage.at[at], relation_out.at[at], out_sems.at[1, c])
        )
        stores[-1].start()
    for c in range(count):
        loads[c].wait()
        at = pl.ds(c * rows, rows)
        stores.append(pltpu.make_async_copy(stage.at[at], entity_out.at[at], out_sems.at[0, c]))
        stores[-1].start()
    for store in stores:
        store.wait()


def local(
    n_ent,
    n_rel,
    entity_rows,
    request_rows,
    edge_heads,
    edge_rels,
    edge_tails,
    edge_counts,
    negative_rows,
    relation_blocks,
):
    entities, width = entity_rows.shape
    slots = request_rows.shape[2]
    slot_total = n_ent * slots
    edges = edge_heads.shape[0]
    negs = negative_rows.shape[0]
    r_count, block_count, block, _ = relation_blocks.shape
    chunk = min(512, edges)
    piece = 128
    pieces = entities // 2 // piece
    stacked = r_count * width
    flat_rows = stacked * block // LANES
    per_owner = flat_rows // n_ent
    wire = BF16 if per_owner % 16 == 0 else F32
    terms = edges + negs + slot_total
    vmem = pltpu.VMEM
    dma = pltpu.SemaphoreType.DMA
    spec = pl.BlockSpec(memory_space=pl.ANY)
    out_shape = (
        jax.ShapeDtypeStruct((2, pieces, piece, width), F32),
        jax.ShapeDtypeStruct((n_ent, per_owner, LANES), wire),
    )
    scratch = [
        pltpu.SMEM((1,), jnp.int32),
        vmem((entities, width), BF16),
        vmem(request_rows.shape, jnp.int32),
        vmem((edges // LANES, LANES), jnp.int32),
        vmem((edges // LANES, LANES), jnp.int32),
        vmem((edges // LANES, LANES), jnp.int32),
        vmem((negs // LANES, LANES), jnp.int32),
        vmem((stacked, block), BF16),
        vmem((2, pieces, piece, width), BF16),
        vmem((2, pieces, piece, width), BF16),
        vmem((n_ent, per_owner, LANES), wire),
        vmem((2, pieces, piece, width), F32),
        vmem((n_ent, LANES), jnp.int32),
        vmem((n_ent, 8, LANES), jnp.int32),
        vmem((n_ent, 8, LANES), jnp.int32),
        vmem((n_ent, slots, width), BF16),
        vmem((n_ent, slots, width), BF16),
        vmem((n_ent, slots, width), BF16),
        vmem((entities, terms), BF16),
        vmem((terms, width), BF16),
        vmem((slot_total, edges), BF16),
        vmem((edges, LANES), jnp.int32),
        vmem((chunk, entities), BF16),
        vmem((stacked, width), BF16),
        vmem((stacked, width), BF16),
        vmem((edges, stacked), BF16),
        vmem((chunk, stacked), BF16),
        vmem((edges, width), BF16),
        vmem((edges, negs), BF16),
        vmem((negs, width), BF16),
        vmem((edges, width), BF16),
        vmem((edges, width), BF16),
        vmem((width, edges), BF16),
        vmem((pieces, piece, width), BF16),
        vmem((pieces, piece, width), BF16),
        vmem((n_ent, per_owner, LANES), wire),
        vmem((n_ent, per_owner, LANES), wire),
        vmem((per_owner, LANES), wire),
        dma((2, n_ent)),
        dma((2, n_ent)),
        dma((2, n_ent)),
        dma((2, pieces)),
        dma((2, pieces)),
        dma((2, pieces)),
        dma((2, pieces)),
        dma((2, n_ent)),
        dma((2, n_ent)),
        dma((8,)),
        dma((2, pieces)),
        dma((1,)),
    ]
    entity_sum, relation_sum = pl.pallas_call(
        functools.partial(kernel, (n_ent, n_rel)),
        out_shape=out_shape,
        in_specs=[spec] * 8,
        out_specs=(spec,) * 2,
        scratch_shapes=scratch,
        compiler_params=pltpu.CompilerParams(
            collective_id=0, has_side_effects=True, vmem_limit_bytes=56 * 1024 * 1024
        ),
    )(
        edge_counts,
        entity_rows,
        request_rows,
        edge_heads.reshape(edges // LANES, LANES),
        edge_rels.reshape(edges // LANES, LANES),
        edge_tails.reshape(edges // LANES, LANES),
        negative_rows.reshape(negs // LANES, LANES),
        relation_blocks.reshape(stacked, block),
    )
    entity_grad, relation_grad = pl.pallas_call(
        finish,
        out_shape=(
            jax.ShapeDtypeStruct((entities, width), F32),
            jax.ShapeDtypeStruct((stacked, block), F32),
        ),
        in_specs=[spec] * 2,
        out_specs=(spec,) * 2,
        scratch_shapes=[
            vmem((flat_rows, LANES), wire),
            vmem((stacked, block), F32),
            vmem((entities, width), F32),
            dma((9,)),
            dma((2, 8)),
        ],
        compiler_params=pltpu.CompilerParams(vmem_limit_bytes=56 * 1024 * 1024),
    )(entity_sum.reshape(entities, width), relation_sum.reshape(flat_rows, LANES))
    return entity_grad, relation_grad.reshape(relation_blocks.shape)


def solution(mesh):
    in_specs = (
        P("ent", None),
        P("ent", None, None),
        P(("ent", "rel")),
        P(("ent", "rel")),
        P(("ent", "rel")),
        P(("ent", "rel")),
        P(("ent", "rel")),
        P("rel", None, None, None),
    )
    out_specs = (P("ent", None), P("rel", None, None, None))
    body = functools.partial(local, mesh.shape["ent"], mesh.shape["rel"])
    return jax.shard_map(body, mesh=mesh, in_specs=in_specs, out_specs=out_specs, check_vma=False)
```

```python
import functools

import jax
import jax.numpy as jnp
from jax import lax
from jax.experimental import pallas as pl
from jax.experimental.pallas import tpu as pltpu
from jax.sharding import PartitionSpec as P

MESH = pl.DeviceIdType.MESH
F32 = jnp.float32
BF16 = jnp.bfloat16
LANES = 128


def iota(shape, axis):
    return lax.broadcasted_iota(jnp.int32, shape, axis)


def hot(mask):
    return jnp.where(mask, 1.0, 0.0).astype(BF16)


def nn(a, b):
    return jnp.dot(a, b, preferred_element_type=F32)


def nt(a, b):
    return lax.dot_general(a, b, (((1,), (1,)), ((), ())), preferred_element_type=F32)


def tn(a, b):
    return lax.dot_general(a, b, (((0,), (0,)), ((), ())), preferred_element_type=F32)


def column(row):
    return jnp.transpose(jnp.broadcast_to(row, (LANES, LANES)))


def each(count, body):
    if count <= 8:
        for step in range(count):
            body(step)
    else:
        lax.fori_loop(0, count, lambda step, _: (body(step), 0)[1], 0)


def kernel(
    dims,
    counts_hbm,
    entity_hbm,
    request_hbm,
    heads_hbm,
    rels_hbm,
    tails_hbm,
    negs_hbm,
    blocks_hbm,
    entity_out,
    relation_out,
    counts_ref,
    entity_ref,
    request_ref,
    heads_ref,
    rels_ref,
    tails_ref,
    negs_ref,
    blocks_ref,
    sum_a_ref,
    sum_b_ref,
    rel_out_ref,
    entity_stage,
    request_wide,
    request_send,
    request_recv,
    want_send,
    fetched,
    slot_send,
    scatter_hot,
    grads,
    tail_hot_t,
    codes,
    hot_rows,
    operators,
    operators_t,
    masked_heads,
    masked_grads,
    projected,
    neg_weight,
    neg_rows,
    weighted,
    grad_proj,
    grad_proj_t,
    part_send,
    part_recv,
    own_half,
    rel_send,
    rel_recv,
    rel_own,
    request_sems,
    fetch_sems,
    slot_sems,
    part_sems,
    cross_sems,
    near_sems,
    far_sems,
    rs_sems,
    ag_sems,
    in_sems,
    entity_sems,
    relation_sems,
):
    n_ent, n_rel = dims
    me, rel = lax.axis_index("ent"), lax.axis_index("rel")
    core, side = rel % 2, rel // 2
    near = side * 2 + (1 - core)
    cross = (1 - side) * 2 + core
    entities, width = entity_ref.shape
    slots = request_ref.shape[2]
    slot_total = n_ent * slots
    edges = heads_ref.shape[0] * LANES
    negs = negs_ref.shape[0] * LANES
    block = blocks_ref.shape[1]
    r_count = blocks_ref.shape[0] // width
    chunk = masked_grads.shape[0]
    chunks = edges // chunk
    piece = sum_a_ref.shape[2]
    per = LANES // slots
    head_bits = (entities - 1).bit_length()
    rel_bits = (r_count - 1).bit_length()
    neg_at, slot_at = edges, edges + negs
    half = entities // 2

    loads = [
        pltpu.make_async_copy(src, dst, in_sems.at[k])
        for k, (src, dst) in enumerate(
            (
                (request_hbm, request_ref),
                (heads_hbm, heads_ref),
                (rels_hbm, rels_ref),
                (tails_hbm, tails_ref),
                (negs_hbm, negs_ref),
                (entity_hbm, entity_ref),
                (blocks_hbm, blocks_ref),
                (counts_hbm, counts_ref),
            )
        )
    ]
    for load in loads:
        load.start()

    barrier = pltpu.get_barrier_semaphore()

    def greet(step):
        pl.semaphore_signal(
            barrier, inc=1, device_id=(lax.rem(me + step + 1, n_ent), rel), device_id_type=MESH
        )

    each(n_ent - 1, greet)
    for partner in (near, cross):
        pl.semaphore_signal(barrier, inc=1, device_id=(me, partner), device_id_type=MESH)

    request_wide[...] = jnp.zeros_like(request_wide)
    loads[0].wait()
    request_wide[:, :slots] = request_ref[0]
    base = request_wide[...]
    wide = base
    for q in range(1, per):
        wide = wide + pltpu.roll(base, q * slots, 1)
    for p in range(n_ent):
        request_send[p] = jnp.broadcast_to(wide[p : p + 1], (8, LANES))
    request_recv[me] = request_send[me]

    for load in loads[1:5]:
        load.wait()
    for k in range(edges // LANES):
        code = heads_ref[k : k + 1] + (
            (rels_ref[k : k + 1] + (tails_ref[k : k + 1] << rel_bits)) << head_bits
        )
        codes[k * LANES : (k + 1) * LANES] = column(code)
    lane = iota((LANES, LANES), 1)
    for k in range(negs // LANES):
        ids = column(negs_ref[k : k + 1])
        for c in range(entities // LANES):
            hot_rows[k * LANES : (k + 1) * LANES, c * LANES : (c + 1) * LANES] = hot(
                ids == lane + c * LANES
            )
    loads[5].wait()
    neg_rows[...] = nn(hot_rows[:negs], entity_ref[...]).astype(BF16)

    pl.semaphore_wait(barrier, n_ent + 1)

    def exchange(src, dst, sems, step):
        target = lax.rem(me + step + 1, n_ent)
        return pltpu.make_async_remote_copy(
            src_ref=src.at[target],
            dst_ref=dst.at[me],
            send_sem=sems.at[0, target],
            recv_sem=sems.at[1, me],
            device_id=(target, rel),
            device_id_type=MESH,
        )

    def arrival(dst, sems, step):
        source = lax.rem(me + step + 1, n_ent)
        return pltpu.make_async_remote_copy(
            src_ref=dst.at[source],
            dst_ref=dst.at[source],
            send_sem=sems.at[0, source],
            recv_sem=sems.at[1, source],
            device_id=(source, rel),
            device_id_type=MESH,
        )

    def start_all(src, dst, sems):
        each(n_ent - 1, lambda step: exchange(src, dst, sems, step).start())

    def wait_all(dst, sems):
        each(n_ent - 1, lambda step: arrival(dst, sems, step).wait_recv())

    def drain_all(src, dst, sems):
        each(n_ent - 1, lambda step: exchange(src, dst, sems, step).wait_send())

    start_all(request_send, request_recv, request_sems)

    spread = hot(iota((block, width), 1) % block == iota((block, width), 0))
    spread_t = hot(iota((width, block), 0) % block == iota((width, block), 1))
    diagonal = iota((width, width), 0) // block == iota((width, width), 1) // block
    loads[6].wait()
    loads[7].wait()
    live_count = counts_ref[0]
    for r in range(r_count):
        rows = slice(r * width, (r + 1) * width)
        one = blocks_ref[rows]
        operators[rows] = jnp.where(diagonal, nn(one, spread), 0.0).astype(BF16)
        operators_t[rows] = jnp.where(diagonal, nt(spread_t, one), 0.0).astype(BF16)

    def rel_masks(rows):
        ids = (codes[rows] >> head_bits) & (r_count - 1)
        return [hot(ids == r) for r in range(r_count)]

    def mask_by_rel(source, masks, target, rows):
        for r in range(r_count):
            for c in range(width // LANES):
                at = r * width + c * LANES
                target[rows, at : at + LANES] = source[:, c * LANES : (c + 1) * LANES] * masks[r]

    wide_lane = iota((chunk, LANES), 1)

    def project(i):
        rows = slice(i * chunk, (i + 1) * chunk)
        ids = codes[rows] & (entities - 1)
        for c in range(entities // LANES):
            hot_rows[:, c * LANES : (c + 1) * LANES] = hot(ids == wide_lane + c * LANES)
        head = nn(hot_rows[...], entity_ref[...]).astype(BF16)
        mask_by_rel(head, rel_masks(rows), masked_heads, rows)
        proj = nn(masked_heads[rows], operators[...]).astype(BF16)
        projected[rows] = proj
        score = nt(proj, neg_rows[...])
        live = iota((chunk, negs), 0) + i * chunk < live_count
        weight = jnp.where(live, jax.nn.sigmoid(score) * (1.0 / negs), 0.0).astype(BF16)
        neg_weight[rows] = weight
        return tn(weight, proj)

    neg_grad = project(0)

    wait_all(request_recv, request_sems)
    request_rows = []
    lane8 = iota((8, LANES), 1) // slots
    for g in range(n_ent // per):
        row = request_recv[g * per]
        for q in range(1, per):
            row = jnp.where(lane8 == q, request_recv[g * per + q], row)
        row = row[:1]
        request_rows.append(row)
        ids = column(row)
        for c in range(entities // LANES):
            hot_rows[:LANES, c * LANES : (c + 1) * LANES] = hot(ids == lane + c * LANES)
        want_send[g * per : (g + 1) * per] = (
            nn(hot_rows[:LANES], entity_ref[...]).astype(BF16).reshape(per, slots, width)
        )
    fetched[me] = want_send[me]
    start_all(want_send, fetched, fetch_sems)

    for i in range(1, chunks):
        neg_grad = neg_grad + project(i)
    grads[neg_at : neg_at + negs] = neg_grad.astype(BF16)

    sub = iota((entities, LANES), 0)
    for k in range(edges // LANES):
        scatter_hot[:, k * LANES : (k + 1) * LANES] = hot(sub == heads_ref[k : k + 1])
    for k in range(negs // LANES):
        at = neg_at + k * LANES
        scatter_hot[:, at : at + LANES] = hot(sub == negs_ref[k : k + 1])
    for k, row in enumerate(request_rows):
        at = slot_at + k * LANES
        scatter_hot[:, at : at + LANES] = hot(sub == row)
    slot_sub = iota((slot_total, LANES), 0)
    for k in range(edges // LANES):
        tail_hot_t[:, k * LANES : (k + 1) * LANES] = hot(slot_sub == tails_ref[k : k + 1])

    wait_all(fetched, fetch_sems)
    table = fetched[...].reshape(slot_total, width)
    for i in range(chunks):
        rows = slice(i * chunk, (i + 1) * chunk)
        ids = codes[rows] >> (head_bits + rel_bits)
        tail_hot = jnp.concatenate(
            [hot(ids == wide_lane + c * LANES) for c in range(slot_total // LANES)], axis=1
        )
        tail = nn(tail_hot, table)
        proj = projected[rows].astype(F32)
        positive = jnp.sum(proj * tail, axis=1, keepdims=True)
        live = iota((chunk, 1), 0) + i * chunk < live_count
        pos_weight = jnp.where(live, -jax.nn.sigmoid(-positive), 0.0)
        weighted[rows] = (pos_weight * proj).astype(BF16)
        grad_proj[rows] = (pos_weight * tail + nn(neg_weight[rows], neg_rows[...])).astype(BF16)
    per_step = min(n_ent, 8)
    for g in range(n_ent // per_step):
        rows = slice(g * per_step * slots, (g + 1) * per_step * slots)
        slot_send[g * per_step : (g + 1) * per_step] = (
            nn(tail_hot_t[rows], weighted[...]).astype(BF16).reshape(per_step, slots, width)
        )
    slot_recv = grads.at[slot_at : slot_at + slot_total]

    def slot_copy(step):
        target = lax.rem(me + step + 1, n_ent)
        return pltpu.make_async_remote_copy(
            src_ref=slot_send.at[target],
            dst_ref=grads.at[pl.ds(pl.multiple_of(slot_at + me * slots, slots), slots)],
            send_sem=slot_sems.at[0, target],
            recv_sem=slot_sems.at[1, me],
            device_id=(target, rel),
            device_id_type=MESH,
        )

    def slot_arrival(step):
        source = lax.rem(me + step + 1, n_ent)
        return pltpu.make_async_remote_copy(
            src_ref=slot_send.at[source],
            dst_ref=grads.at[pl.ds(pl.multiple_of(slot_at + source * slots, slots), slots)],
            send_sem=slot_sems.at[0, source],
            recv_sem=slot_sems.at[1, source],
            device_id=(source, rel),
            device_id_type=MESH,
        )

    each(n_ent - 1, lambda step: slot_copy(step).start())
    grads[pl.ds(pl.multiple_of(slot_at + me * slots, slots), slots)] = slot_send[me]

    wire = rel_send.dtype
    per_owner = rel_send.shape[1]
    grad_proj_t[...] = jnp.transpose(grad_proj[...])
    block_of_lane = iota((block, width), 1) // block
    step_rows = min(block, per_owner)
    def relation_terms(first, last):
        for r in range(first, last):
            outer = nn(grad_proj_t[...], masked_heads[:, r * width : (r + 1) * width])
            small = jnp.zeros((block, width), F32)
            for n in range(width // block):
                small = small + jnp.where(
                    block_of_lane == n, outer[n * block : (n + 1) * block], 0.0
                )
            for c in range(width // LANES):
                for t in range(block // step_rows):
                    flat = (r * (width // LANES) + c) * block + t * step_rows
                    owner, at = flat // per_owner, flat % per_owner
                    rel_send[owner, at : at + step_rows] = small[
                        t * step_rows : (t + 1) * step_rows, c * LANES : (c + 1) * LANES
                    ].astype(wire)

    relation_terms(0, r_count)
    start_all(rel_send, rel_recv, rs_sems)
    rel_recv[me] = rel_send[me]

    for i in range(chunks):
        rows = slice(i * chunk, (i + 1) * chunk)
        mask_by_rel(grad_proj[rows], rel_masks(rows), masked_grads, slice(0, chunk))
        grads[rows] = nn(masked_grads[...], operators_t[...]).astype(BF16)

    each(n_ent - 1, lambda step: slot_arrival(step).wait_recv())

    pieces = half // piece
    pair = 2
    part_copies, cross_copies, near_copies, far_copies = [], [], [], []

    def near_copy(src, dst, sems, q, target):
        copy = pltpu.make_async_remote_copy(
            src_ref=src,
            dst_ref=dst,
            send_sem=sems.at[0, q],
            recv_sem=sems.at[1, q],
            device_id=(me, target),
            device_id_type=MESH,
        )
        copy.start()
        return copy

    for g in range(pieces // pair):
        at = pl.multiple_of((1 - core) * half + g * pair * piece, pair * piece)
        part = nn(scatter_hot[pl.ds(at, pair * piece)], grads[...]).astype(BF16)
        for q in range(g * pair, (g + 1) * pair):
            low = (q - g * pair) * piece
            part_send[q] = part[low : low + piece]
            part_copies.append(near_copy(part_send.at[q], part_recv.at[q], part_sems, q, near))
    for g in range(pieces // pair):
        at = pl.multiple_of(core * half + g * pair * piece, pair * piece)
        own_half[g] = nn(scatter_hot[pl.ds(at, pair * piece)], grads[...])
    wait_all(rel_recv, rs_sems)
    total = rel_recv[0].astype(F32)
    for p in range(1, n_ent):
        total = total + rel_recv[p].astype(F32)
    rel_own[...] = total.astype(wire)
    rel_out_ref[me] = rel_own[...]

    def gather_copy(step):
        target = lax.rem(me + step + 1, n_ent)
        return pltpu.make_async_remote_copy(
            src_ref=rel_own,
            dst_ref=rel_out_ref.at[me],
            send_sem=ag_sems.at[0, target],
            recv_sem=ag_sems.at[1, me],
            device_id=(target, rel),
            device_id_type=MESH,
        )

    each(n_ent - 1, lambda step: gather_copy(step).start())
    for g in range(pieces // pair):
        own = own_half[g]
        for q in range(g * pair, (g + 1) * pair):
            low = (q - g * pair) * piece
            part_copies[q].wait_recv()
            sum_a_ref[core, q] = (own[low : low + piece] + part_recv[q].astype(F32)).astype(BF16)
            mine = sum_a_ref.at[core, q]
            cross_copies.append(near_copy(mine, sum_b_ref.at[core, q], cross_sems, q, cross))
            near_copies.append(near_copy(mine, mine, near_sems, q, near))

    def write_entity(which, q):
        entity_stage[which, q] = sum_a_ref[which, q].astype(F32) + sum_b_ref[which, q].astype(F32)
        copy = pltpu.make_async_copy(
            entity_stage.at[which, q], entity_out.at[which, q], entity_sems.at[which, q]
        )
        copy.start()
        return copy

    stores = []

    def forward(q):
        cross_copies[q].wait_recv()
        theirs = sum_b_ref.at[core, q]
        far_copies.append(near_copy(theirs, theirs, far_sems, q, near))
        stores.append(write_entity(core, q))

    def finish_other(q):
        near_copies[q].wait_recv()
        far_copies[q].wait_recv()
        stores.append(write_entity(1 - core, q))

    for q in range(pieces - 1):
        forward(q)
    wait_all(rel_out_ref, ag_sems)
    copy = pltpu.make_async_copy(rel_out_ref, relation_out, relation_sems.at[0])
    copy.start()
    stores.append(copy)
    for q in range(pieces - 1):
        finish_other(q)
    forward(pieces - 1)
    finish_other(pieces - 1)
    for copy in stores:
        copy.wait()
    drain_all(request_send, request_recv, request_sems)
    drain_all(want_send, fetched, fetch_sems)
    each(n_ent - 1, lambda step: slot_copy(step).wait_send())
    drain_all(rel_send, rel_recv, rs_sems)
    each(n_ent - 1, lambda step: gather_copy(step).wait_send())
    for copies in (part_copies, cross_copies, near_copies, far_copies):
        for copy in copies:
            copy.wait_send()


def finish(
    entity_ref, relation_ref, entity_out, relation_out, rel_in, rel_stage, stage, in_sems, out_sems
):
    count = out_sems.shape[1]
    rows = stage.shape[0] // count
    tall = rel_stage.shape[0] // count
    block = rel_stage.shape[1]
    rel_load = pltpu.make_async_copy(relation_ref, rel_in, in_sems.at[count])
    rel_load.start()
    loads, stores = [], []
    for c in range(count):
        at = pl.ds(c * rows, rows)
        loads.append(pltpu.make_async_copy(entity_ref.at[at], stage.at[at], in_sems.at[c]))
        loads[c].start()
    rel_load.wait()
    for c in range(count):
        for k in range(c * tall // LANES, (c + 1) * tall // LANES):
            rel_stage[k * LANES : (k + 1) * LANES] = jnp.transpose(
                rel_in[k * block : (k + 1) * block].astype(F32)
            )
        at = pl.ds(c * tall, tall)
        stores.append(
            pltpu.make_async_copy(rel_stage.at[at], relation_out.at[at], out_sems.at[1, c])
        )
        stores[-1].start()
    for c in range(count):
        loads[c].wait()
        at = pl.ds(c * rows, rows)
        stores.append(pltpu.make_async_copy(stage.at[at], entity_out.at[at], out_sems.at[0, c]))
        stores[-1].start()
    for store in stores:
        store.wait()


def local(
    n_ent,
    n_rel,
    entity_rows,
    request_rows,
    edge_heads,
    edge_rels,
    edge_tails,
    edge_counts,
    negative_rows,
    relation_blocks,
):
    entities, width = entity_rows.shape
    slots = request_rows.shape[2]
    slot_total = n_ent * slots
    edges = edge_heads.shape[0]
    negs = negative_rows.shape[0]
    r_count, block_count, block, _ = relation_blocks.shape
    chunk = min(512, edges)
    piece = 128
    pieces = entities // 2 // piece
    stacked = r_count * width
    flat_rows = stacked * block // LANES
    per_owner = flat_rows // n_ent
    wire = BF16 if per_owner % 16 == 0 else F32
    terms = edges + negs + slot_total
    vmem = pltpu.VMEM
    dma = pltpu.SemaphoreType.DMA
    spec = pl.BlockSpec(memory_space=pltpu.HBM)
    out_shape = (
        jax.ShapeDtypeStruct((2, pieces, piece, width), F32),
        jax.ShapeDtypeStruct((n_ent, per_owner, LANES), wire),
    )
    scratch = [
        pltpu.SMEM((1,), jnp.int32),
        vmem((entities, width), BF16),
        vmem(request_rows.shape, jnp.int32),
        vmem((edges // LANES, LANES), jnp.int32),
        vmem((edges // LANES, LANES), jnp.int32),
        vmem((edges // LANES, LANES), jnp.int32),
        vmem((negs // LANES, LANES), jnp.int32),
        vmem((stacked, block), BF16),
        vmem((2, pieces, piece, width), BF16),
        vmem((2, pieces, piece, width), BF16),
        vmem((n_ent, per_owner, LANES), wire),
        vmem((2, pieces, piece, width), F32),
        vmem((n_ent, LANES), jnp.int32),
        vmem((n_ent, 8, LANES), jnp.int32),
        vmem((n_ent, 8, LANES), jnp.int32),
        vmem((n_ent, slots, width), BF16),
        vmem((n_ent, slots, width), BF16),
        vmem((n_ent, slots, width), BF16),
        vmem((entities, terms), BF16),
        vmem((terms, width), BF16),
        vmem((slot_total, edges), BF16),
        vmem((edges, LANES), jnp.int32),
        vmem((chunk, entities), BF16),
        vmem((stacked, width), BF16),
        vmem((stacked, width), BF16),
        vmem((edges, stacked), BF16),
        vmem((chunk, stacked), BF16),
        vmem((edges, width), BF16),
        vmem((edges, negs), BF16),
        vmem((negs, width), BF16),
        vmem((edges, width), BF16),
        vmem((edges, width), BF16),
        vmem((width, edges), BF16),
        vmem((pieces, piece, width), BF16),
        vmem((pieces, piece, width), BF16),
        vmem((pieces // 2, 2 * piece, width), F32),
        vmem((n_ent, per_owner, LANES), wire),
        vmem((n_ent, per_owner, LANES), wire),
        vmem((per_owner, LANES), wire),
        dma((2, n_ent)),
        dma((2, n_ent)),
        dma((2, n_ent)),
        dma((2, pieces)),
        dma((2, pieces)),
        dma((2, pieces)),
        dma((2, pieces)),
        dma((2, n_ent)),
        dma((2, n_ent)),
        dma((8,)),
        dma((2, pieces)),
        dma((1,)),
    ]
    entity_sum, relation_sum = pl.pallas_call(
        functools.partial(kernel, (n_ent, n_rel)),
        out_shape=out_shape,
        in_specs=[spec] * 8,
        out_specs=(spec,) * 2,
        scratch_shapes=scratch,
        compiler_params=pltpu.CompilerParams(
            collective_id=0, has_side_effects=True, vmem_limit_bytes=56 * 1024 * 1024
        ),
    )(
        edge_counts,
        entity_rows,
        request_rows,
        edge_heads.reshape(edges // LANES, LANES),
        edge_rels.reshape(edges // LANES, LANES),
        edge_tails.reshape(edges // LANES, LANES),
        negative_rows.reshape(negs // LANES, LANES),
        relation_blocks.reshape(stacked, block),
    )
    entity_grad, relation_grad = pl.pallas_call(
        finish,
        out_shape=(
            jax.ShapeDtypeStruct((entities, width), F32),
            jax.ShapeDtypeStruct((stacked, block), F32),
        ),
        in_specs=[spec] * 2,
        out_specs=(spec,) * 2,
        scratch_shapes=[
            vmem((flat_rows, LANES), wire),
            vmem((stacked, block), F32),
            vmem((entities, width), F32),
            dma((9,)),
            dma((2, 8)),
        ],
        compiler_params=pltpu.CompilerParams(vmem_limit_bytes=56 * 1024 * 1024),
    )(entity_sum.reshape(entities, width), relation_sum.reshape(flat_rows, LANES))
    return entity_grad, relation_grad.reshape(relation_blocks.shape)


def solution(mesh):
    in_specs = (
        P("ent", None),
        P("ent", None, None),
        P(("ent", "rel")),
        P(("ent", "rel")),
        P(("ent", "rel")),
        P(("ent", "rel")),
        P(("ent", "rel")),
        P("rel", None, None, None),
    )
    out_specs = (P("ent", None), P("rel", None, None, None))
    body = functools.partial(local, mesh.shape["ent"], mesh.shape["rel"])
    return jax.shard_map(body, mesh=mesh, in_specs=in_specs, out_specs=out_specs, check_vma=False)
```

```python
import functools

import jax
import jax.numpy as jnp
from jax import lax
from jax.experimental import pallas as pl
from jax.experimental.pallas import tpu as pltpu
from jax.sharding import PartitionSpec as P

MESH = pl.DeviceIdType.MESH
F32 = jnp.float32
BF16 = jnp.bfloat16
LANES = 128


def iota(shape, axis):
    return lax.broadcasted_iota(jnp.int32, shape, axis)


def hot(mask):
    return jnp.where(mask, 1.0, 0.0).astype(BF16)


def nn(a, b):
    return jnp.dot(a, b, preferred_element_type=F32)


def nt(a, b):
    return lax.dot_general(a, b, (((1,), (1,)), ((), ())), preferred_element_type=F32)


def tn(a, b):
    return lax.dot_general(a, b, (((0,), (0,)), ((), ())), preferred_element_type=F32)


def column(row):
    return jnp.transpose(jnp.broadcast_to(row, (LANES, LANES)))


def each(count, body):
    if count <= 8:
        for step in range(count):
            body(step)
    else:
        lax.fori_loop(0, count, lambda step, _: (body(step), 0)[1], 0)


def kernel(
    dims,
    counts_hbm,
    entity_hbm,
    request_hbm,
    heads_hbm,
    rels_hbm,
    tails_hbm,
    negs_hbm,
    blocks_hbm,
    entity_out,
    relation_out,
    counts_ref,
    entity_ref,
    request_ref,
    heads_ref,
    rels_ref,
    tails_ref,
    negs_ref,
    blocks_ref,
    sum_a_ref,
    sum_b_ref,
    rel_out_ref,
    entity_stage,
    request_wide,
    request_send,
    request_recv,
    want_send,
    fetched,
    slot_send,
    scatter_hot,
    grads,
    tail_hot_t,
    codes,
    hot_rows,
    operators,
    operators_t,
    masked_heads,
    masked_grads,
    projected,
    neg_weight,
    neg_rows,
    weighted,
    grad_proj,
    grad_proj_t,
    part_send,
    part_recv,
    own_half,
    rel_send,
    rel_recv,
    rel_own,
    request_sems,
    fetch_sems,
    slot_sems,
    part_sems,
    cross_sems,
    near_sems,
    far_sems,
    rs_sems,
    ag_sems,
    in_sems,
    entity_sems,
    relation_sems,
):
    n_ent, n_rel = dims
    me, rel = lax.axis_index("ent"), lax.axis_index("rel")
    core, side = rel % 2, rel // 2
    near = side * 2 + (1 - core)
    cross = (1 - side) * 2 + core
    entities, width = entity_ref.shape
    slots = request_ref.shape[2]
    slot_total = n_ent * slots
    edges = heads_ref.shape[0] * LANES
    negs = negs_ref.shape[0] * LANES
    block = blocks_ref.shape[1]
    r_count = blocks_ref.shape[0] // width
    chunk = hot_rows.shape[0]
    chunks = edges // chunk
    piece = sum_a_ref.shape[2]
    per = LANES // slots
    head_bits = (entities - 1).bit_length()
    rel_bits = (r_count - 1).bit_length()
    neg_at, slot_at = edges, edges + negs
    half = entities // 2

    loads = [
        pltpu.make_async_copy(src, dst, in_sems.at[k])
        for k, (src, dst) in enumerate(
            (
                (request_hbm, request_ref),
                (heads_hbm, heads_ref),
                (rels_hbm, rels_ref),
                (tails_hbm, tails_ref),
                (negs_hbm, negs_ref),
                (entity_hbm, entity_ref),
                (blocks_hbm, blocks_ref),
                (counts_hbm, counts_ref),
            )
        )
    ]
    for load in loads:
        load.start()

    barrier = pltpu.get_barrier_semaphore()

    def greet(step):
        pl.semaphore_signal(
            barrier, inc=1, device_id=(lax.rem(me + step + 1, n_ent), rel), device_id_type=MESH
        )

    each(n_ent - 1, greet)
    for partner in (near, cross):
        pl.semaphore_signal(barrier, inc=1, device_id=(me, partner), device_id_type=MESH)

    request_wide[...] = jnp.zeros_like(request_wide)
    loads[0].wait()
    request_wide[:, :slots] = request_ref[0]
    base = request_wide[...]
    wide = base
    for q in range(1, per):
        wide = wide + pltpu.roll(base, q * slots, 1)
    for p in range(n_ent):
        request_send[p] = jnp.broadcast_to(wide[p : p + 1], (8, LANES))
    request_recv[me] = request_send[me]

    for load in loads[1:5]:
        load.wait()
    for k in range(edges // LANES):
        code = heads_ref[k : k + 1] + (
            (rels_ref[k : k + 1] + (tails_ref[k : k + 1] << rel_bits)) << head_bits
        )
        codes[k * LANES : (k + 1) * LANES] = column(code)
    lane = iota((LANES, LANES), 1)
    for k in range(negs // LANES):
        ids = column(negs_ref[k : k + 1])
        for c in range(entities // LANES):
            hot_rows[k * LANES : (k + 1) * LANES, c * LANES : (c + 1) * LANES] = hot(
                ids == lane + c * LANES
            )
    loads[5].wait()
    neg_rows[...] = nn(hot_rows[:negs], entity_ref[...]).astype(BF16)

    pl.semaphore_wait(barrier, n_ent + 1)

    def exchange(src, dst, sems, step):
        target = lax.rem(me + step + 1, n_ent)
        return pltpu.make_async_remote_copy(
            src_ref=src.at[target],
            dst_ref=dst.at[me],
            send_sem=sems.at[0, target],
            recv_sem=sems.at[1, me],
            device_id=(target, rel),
            device_id_type=MESH,
        )

    def arrival(dst, sems, step):
        source = lax.rem(me + step + 1, n_ent)
        return pltpu.make_async_remote_copy(
            src_ref=dst.at[source],
            dst_ref=dst.at[source],
            send_sem=sems.at[0, source],
            recv_sem=sems.at[1, source],
            device_id=(source, rel),
            device_id_type=MESH,
        )

    def start_all(src, dst, sems):
        each(n_ent - 1, lambda step: exchange(src, dst, sems, step).start())

    def wait_all(dst, sems):
        each(n_ent - 1, lambda step: arrival(dst, sems, step).wait_recv())

    def drain_all(src, dst, sems):
        each(n_ent - 1, lambda step: exchange(src, dst, sems, step).wait_send())

    start_all(request_send, request_recv, request_sems)

    spread = hot(iota((block, width), 1) % block == iota((block, width), 0))
    spread_t = hot(iota((width, block), 0) % block == iota((width, block), 1))
    diagonal = iota((width, width), 0) // block == iota((width, width), 1) // block
    loads[6].wait()
    loads[7].wait()
    live_count = counts_ref[0]
    for r in range(r_count):
        rows = slice(r * width, (r + 1) * width)
        one = blocks_ref[rows]
        plain = jnp.where(diagonal, nn(one, spread), 0.0).astype(BF16)
        turned = jnp.where(diagonal, nt(spread_t, one), 0.0).astype(BF16)
        for c in range(width // LANES):
            part = slice(c * LANES, (c + 1) * LANES)
            at = (c * r_count + r) * LANES
            operators[at : at + LANES] = plain[part]
            operators_t[at : at + LANES] = turned[part]

    def rel_masks(rows):
        ids = (codes[rows] >> head_bits) & (r_count - 1)
        return [hot(ids == r) for r in range(r_count)]

    def mask_by_rel(source, masks, target, rows):
        for r in range(r_count):
            for c in range(width // LANES):
                at = (c * r_count + r) * LANES
                target[rows, at : at + LANES] = source[:, c * LANES : (c + 1) * LANES] * masks[r]

    wide_lane = iota((chunk, LANES), 1)

    def project(i):
        rows = slice(i * chunk, (i + 1) * chunk)
        ids = codes[rows] & (entities - 1)
        for c in range(entities // LANES):
            hot_rows[:, c * LANES : (c + 1) * LANES] = hot(ids == wide_lane + c * LANES)
        head = nn(hot_rows[...], entity_ref[...]).astype(BF16)
        mask_by_rel(head, rel_masks(rows), masked_heads, rows)
        proj = nn(masked_heads[rows], operators[...]).astype(BF16)
        projected[rows] = proj
        score = nt(proj, neg_rows[...])
        live = iota((chunk, negs), 0) + i * chunk < live_count
        weight = jnp.where(live, jax.nn.sigmoid(score) * (1.0 / negs), 0.0).astype(BF16)
        neg_weight[rows] = weight
        return tn(weight, proj)

    neg_grad = project(0)

    wait_all(request_recv, request_sems)
    request_rows = []
    lane8 = iota((8, LANES), 1) // slots
    for g in range(n_ent // per):
        row = request_recv[g * per]
        for q in range(1, per):
            row = jnp.where(lane8 == q, request_recv[g * per + q], row)
        row = row[:1]
        request_rows.append(row)
        ids = column(row)
        for c in range(entities // LANES):
            hot_rows[:LANES, c * LANES : (c + 1) * LANES] = hot(ids == lane + c * LANES)
        want_send[g * per : (g + 1) * per] = (
            nn(hot_rows[:LANES], entity_ref[...]).astype(BF16).reshape(per, slots, width)
        )
    fetched[me] = want_send[me]
    start_all(want_send, fetched, fetch_sems)

    for i in range(1, chunks):
        neg_grad = neg_grad + project(i)
    grads[neg_at : neg_at + negs] = neg_grad.astype(BF16)

    sub = iota((entities, LANES), 0)
    for k in range(edges // LANES):
        scatter_hot[:, k * LANES : (k + 1) * LANES] = hot(sub == heads_ref[k : k + 1])
    for k in range(negs // LANES):
        at = neg_at + k * LANES
        scatter_hot[:, at : at + LANES] = hot(sub == negs_ref[k : k + 1])
    for k, row in enumerate(request_rows):
        at = slot_at + k * LANES
        scatter_hot[:, at : at + LANES] = hot(sub == row)
    slot_sub = iota((slot_total, LANES), 0)
    for k in range(edges // LANES):
        tail_hot_t[:, k * LANES : (k + 1) * LANES] = hot(slot_sub == tails_ref[k : k + 1])

    wait_all(fetched, fetch_sems)
    table = fetched[...].reshape(slot_total, width)
    for i in range(chunks):
        rows = slice(i * chunk, (i + 1) * chunk)
        ids = codes[rows] >> (head_bits + rel_bits)
        tail_hot = jnp.concatenate(
            [hot(ids == wide_lane + c * LANES) for c in range(slot_total // LANES)], axis=1
        )
        tail = nn(tail_hot, table)
        proj = projected[rows].astype(F32)
        positive = jnp.sum(proj * tail, axis=1, keepdims=True)
        live = iota((chunk, 1), 0) + i * chunk < live_count
        pos_weight = jnp.where(live, -jax.nn.sigmoid(-positive), 0.0)
        weighted[rows] = (pos_weight * proj).astype(BF16)
        grad_proj[rows] = (pos_weight * tail + nn(neg_weight[rows], neg_rows[...])).astype(BF16)
    per_step = min(n_ent, 8)
    for g in range(n_ent // per_step):
        rows = slice(g * per_step * slots, (g + 1) * per_step * slots)
        slot_send[g * per_step : (g + 1) * per_step] = (
            nn(tail_hot_t[rows], weighted[...]).astype(BF16).reshape(per_step, slots, width)
        )
    slot_recv = grads.at[slot_at : slot_at + slot_total]

    def slot_copy(step):
        target = lax.rem(me + step + 1, n_ent)
        return pltpu.make_async_remote_copy(
            src_ref=slot_send.at[target],
            dst_ref=grads.at[pl.ds(pl.multiple_of(slot_at + me * slots, slots), slots)],
            send_sem=slot_sems.at[0, target],
            recv_sem=slot_sems.at[1, me],
            device_id=(target, rel),
            device_id_type=MESH,
        )

    def slot_arrival(step):
        source = lax.rem(me + step + 1, n_ent)
        return pltpu.make_async_remote_copy(
            src_ref=slot_send.at[source],
            dst_ref=grads.at[pl.ds(pl.multiple_of(slot_at + source * slots, slots), slots)],
            send_sem=slot_sems.at[0, source],
            recv_sem=slot_sems.at[1, source],
            device_id=(source, rel),
            device_id_type=MESH,
        )

    each(n_ent - 1, lambda step: slot_copy(step).start())
    grads[pl.ds(pl.multiple_of(slot_at + me * slots, slots), slots)] = slot_send[me]

    wire = rel_send.dtype
    per_owner = rel_send.shape[1]
    grad_proj_t[...] = jnp.transpose(grad_proj[...])
    step_rows = min(block, per_owner)
    span = r_count * LANES
    block_of_lane = iota((block, span), 1) // block % (LANES // block)
    for c in range(width // LANES):
        outer = nn(
            grad_proj_t[c * LANES : (c + 1) * LANES], masked_heads[:, c * span : (c + 1) * span]
        )
        small = jnp.zeros((block, span), F32)
        for n in range(LANES // block):
            small = jnp.where(block_of_lane == n, outer[n * block : (n + 1) * block], small)
        for r in range(r_count):
            for t in range(block // step_rows):
                flat = (r * (width // LANES) + c) * block + t * step_rows
                owner, at = flat // per_owner, flat % per_owner
                rel_send[owner, at : at + step_rows] = small[
                    t * step_rows : (t + 1) * step_rows, r * LANES : (r + 1) * LANES
                ].astype(wire)
    start_all(rel_send, rel_recv, rs_sems)
    rel_recv[me] = rel_send[me]

    for i in range(chunks):
        rows = slice(i * chunk, (i + 1) * chunk)
        mask_by_rel(grad_proj[rows], rel_masks(rows), masked_grads, rows)
    grads[:edges] = nn(masked_grads[...], operators_t[...]).astype(BF16)

    each(n_ent - 1, lambda step: slot_arrival(step).wait_recv())

    pieces = half // piece
    pair = pieces
    part_copies, cross_copies, near_copies, far_copies = [], [], [], []

    def near_copy(src, dst, sems, q, target):
        copy = pltpu.make_async_remote_copy(
            src_ref=src,
            dst_ref=dst,
            send_sem=sems.at[0, q],
            recv_sem=sems.at[1, q],
            device_id=(me, target),
            device_id_type=MESH,
        )
        copy.start()
        return copy

    for g in range(pieces // pair):
        at = pl.multiple_of((1 - core) * half + g * pair * piece, pair * piece)
        part = nn(scatter_hot[pl.ds(at, pair * piece)], grads[...]).astype(BF16)
        for q in range(g * pair, (g + 1) * pair):
            low = (q - g * pair) * piece
            part_send[q] = part[low : low + piece]
            part_copies.append(near_copy(part_send.at[q], part_recv.at[q], part_sems, q, near))
    for g in range(pieces // pair):
        at = pl.multiple_of(core * half + g * pair * piece, pair * piece)
        own_half[g] = nn(scatter_hot[pl.ds(at, pair * piece)], grads[...])
    wait_all(rel_recv, rs_sems)
    total = rel_recv[0].astype(F32)
    for p in range(1, n_ent):
        total = total + rel_recv[p].astype(F32)
    rel_own[...] = total.astype(wire)
    rel_out_ref[me] = rel_own[...]

    def gather_copy(step):
        target = lax.rem(me + step + 1, n_ent)
        return pltpu.make_async_remote_copy(
            src_ref=rel_own,
            dst_ref=rel_out_ref.at[me],
            send_sem=ag_sems.at[0, target],
            recv_sem=ag_sems.at[1, me],
            device_id=(target, rel),
            device_id_type=MESH,
        )

    each(n_ent - 1, lambda step: gather_copy(step).start())
    for g in range(pieces // pair):
        own = own_half[g]
        for q in range(g * pair, (g + 1) * pair):
            low = (q - g * pair) * piece
            part_copies[q].wait_recv()
            sum_a_ref[core, q] = (own[low : low + piece] + part_recv[q].astype(F32)).astype(BF16)
            mine = sum_a_ref.at[core, q]
            cross_copies.append(near_copy(mine, sum_b_ref.at[core, q], cross_sems, q, cross))
            near_copies.append(near_copy(mine, mine, near_sems, q, near))

    def write_entity(which, q):
        entity_stage[which, q] = sum_a_ref[which, q].astype(F32) + sum_b_ref[which, q].astype(F32)
        copy = pltpu.make_async_copy(
            entity_stage.at[which, q], entity_out.at[which, q], entity_sems.at[which, q]
        )
        copy.start()
        return copy

    stores = []

    def forward(q):
        cross_copies[q].wait_recv()
        theirs = sum_b_ref.at[core, q]
        far_copies.append(near_copy(theirs, theirs, far_sems, q, near))
        stores.append(write_entity(core, q))

    def finish_other(q):
        near_copies[q].wait_recv()
        far_copies[q].wait_recv()
        stores.append(write_entity(1 - core, q))

    for q in range(pieces - 1):
        forward(q)
    wait_all(rel_out_ref, ag_sems)
    copy = pltpu.make_async_copy(rel_out_ref, relation_out, relation_sems.at[0])
    copy.start()
    stores.append(copy)
    for q in range(pieces - 1):
        finish_other(q)
    forward(pieces - 1)
    finish_other(pieces - 1)
    for copy in stores:
        copy.wait()
    drain_all(request_send, request_recv, request_sems)
    drain_all(want_send, fetched, fetch_sems)
    each(n_ent - 1, lambda step: slot_copy(step).wait_send())
    drain_all(rel_send, rel_recv, rs_sems)
    each(n_ent - 1, lambda step: gather_copy(step).wait_send())
    for copies in (part_copies, cross_copies, near_copies, far_copies):
        for copy in copies:
            copy.wait_send()


def finish(
    entity_ref, relation_ref, entity_out, relation_out, rel_in, rel_stage, stage, in_sems, out_sems
):
    count = out_sems.shape[1]
    rows = stage.shape[0] // count
    tall = rel_stage.shape[0] // count
    block = rel_stage.shape[1]
    rel_load = pltpu.make_async_copy(relation_ref, rel_in, in_sems.at[count])
    rel_load.start()
    loads, stores = [], []
    for c in range(count):
        at = pl.ds(c * rows, rows)
        loads.append(pltpu.make_async_copy(entity_ref.at[at], stage.at[at], in_sems.at[c]))
        loads[c].start()
    rel_load.wait()
    for c in range(count):
        for k in range(c * tall // LANES, (c + 1) * tall // LANES):
            rel_stage[k * LANES : (k + 1) * LANES] = jnp.transpose(
                rel_in[k * block : (k + 1) * block].astype(F32)
            )
        at = pl.ds(c * tall, tall)
        stores.append(
            pltpu.make_async_copy(rel_stage.at[at], relation_out.at[at], out_sems.at[1, c])
        )
        stores[-1].start()
    for c in range(count):
        loads[c].wait()
        at = pl.ds(c * rows, rows)
        stores.append(pltpu.make_async_copy(stage.at[at], entity_out.at[at], out_sems.at[0, c]))
        stores[-1].start()
    for store in stores:
        store.wait()


def local(
    n_ent,
    n_rel,
    entity_rows,
    request_rows,
    edge_heads,
    edge_rels,
    edge_tails,
    edge_counts,
    negative_rows,
    relation_blocks,
):
    entities, width = entity_rows.shape
    slots = request_rows.shape[2]
    slot_total = n_ent * slots
    edges = edge_heads.shape[0]
    negs = negative_rows.shape[0]
    r_count, block_count, block, _ = relation_blocks.shape
    chunk = min(512, edges)
    piece = 128
    pieces = entities // 2 // piece
    stacked = r_count * width
    flat_rows = stacked * block // LANES
    per_owner = flat_rows // n_ent
    wire = BF16 if per_owner % 16 == 0 else F32
    terms = edges + negs + slot_total
    vmem = pltpu.VMEM
    dma = pltpu.SemaphoreType.DMA
    spec = pl.BlockSpec(memory_space=pltpu.HBM)
    out_shape = (
        jax.ShapeDtypeStruct((2, pieces, piece, width), F32),
        jax.ShapeDtypeStruct((n_ent, per_owner, LANES), wire),
    )
    scratch = [
        pltpu.SMEM((1,), jnp.int32),
        vmem((entities, width), BF16),
        vmem(request_rows.shape, jnp.int32),
        vmem((edges // LANES, LANES), jnp.int32),
        vmem((edges // LANES, LANES), jnp.int32),
        vmem((edges // LANES, LANES), jnp.int32),
        vmem((negs // LANES, LANES), jnp.int32),
        vmem((stacked, block), BF16),
        vmem((2, pieces, piece, width), BF16),
        vmem((2, pieces, piece, width), BF16),
        vmem((n_ent, per_owner, LANES), wire),
        vmem((2, pieces, piece, width), F32),
        vmem((n_ent, LANES), jnp.int32),
        vmem((n_ent, 8, LANES), jnp.int32),
        vmem((n_ent, 8, LANES), jnp.int32),
        vmem((n_ent, slots, width), BF16),
        vmem((n_ent, slots, width), BF16),
        vmem((n_ent, slots, width), BF16),
        vmem((entities, terms), BF16),
        vmem((terms, width), BF16),
        vmem((slot_total, edges), BF16),
        vmem((edges, LANES), jnp.int32),
        vmem((chunk, entities), BF16),
        vmem((stacked, width), BF16),
        vmem((stacked, width), BF16),
        vmem((edges, stacked), BF16),
        vmem((edges, stacked), BF16),
        vmem((edges, width), BF16),
        vmem((edges, negs), BF16),
        vmem((negs, width), BF16),
        vmem((edges, width), BF16),
        vmem((edges, width), BF16),
        vmem((width, edges), BF16),
        vmem((pieces, piece, width), BF16),
        vmem((pieces, piece, width), BF16),
        vmem((1, pieces * piece, width), F32),
        vmem((n_ent, per_owner, LANES), wire),
        vmem((n_ent, per_owner, LANES), wire),
        vmem((per_owner, LANES), wire),
        dma((2, n_ent)),
        dma((2, n_ent)),
        dma((2, n_ent)),
        dma((2, pieces)),
        dma((2, pieces)),
        dma((2, pieces)),
        dma((2, pieces)),
        dma((2, n_ent)),
        dma((2, n_ent)),
        dma((8,)),
        dma((2, pieces)),
        dma((1,)),
    ]
    entity_sum, relation_sum = pl.pallas_call(
        functools.partial(kernel, (n_ent, n_rel)),
        out_shape=out_shape,
        in_specs=[spec] * 8,
        out_specs=(spec,) * 2,
        scratch_shapes=scratch,
        compiler_params=pltpu.CompilerParams(
            collective_id=0, has_side_effects=True, vmem_limit_bytes=56 * 1024 * 1024
        ),
    )(
        edge_counts,
        entity_rows,
        request_rows,
        edge_heads.reshape(edges // LANES, LANES),
        edge_rels.reshape(edges // LANES, LANES),
        edge_tails.reshape(edges // LANES, LANES),
        negative_rows.reshape(negs // LANES, LANES),
        relation_blocks.reshape(stacked, block),
    )
    entity_grad, relation_grad = pl.pallas_call(
        finish,
        out_shape=(
            jax.ShapeDtypeStruct((entities, width), F32),
            jax.ShapeDtypeStruct((stacked, block), F32),
        ),
        in_specs=[spec] * 2,
        out_specs=(spec,) * 2,
        scratch_shapes=[
            vmem((flat_rows, LANES), wire),
            vmem((stacked, block), F32),
            vmem((entities, width), F32),
            dma((9,)),
            dma((2, 8)),
        ],
        compiler_params=pltpu.CompilerParams(vmem_limit_bytes=56 * 1024 * 1024),
    )(entity_sum.reshape(entities, width), relation_sum.reshape(flat_rows, LANES))
    return entity_grad, relation_grad.reshape(relation_blocks.shape)


def solution(mesh):
    in_specs = (
        P("ent", None),
        P("ent", None, None),
        P(("ent", "rel")),
        P(("ent", "rel")),
        P(("ent", "rel")),
        P(("ent", "rel")),
        P(("ent", "rel")),
        P("rel", None, None, None),
    )
    out_specs = (P("ent", None), P("rel", None, None, None))
    body = functools.partial(local, mesh.shape["ent"], mesh.shape["rel"])
    return jax.shard_map(body, mesh=mesh, in_specs=in_specs, out_specs=out_specs, check_vma=False)
```

```python
import functools

import jax
import jax.numpy as jnp
from jax import lax
from jax.experimental import pallas as pl
from jax.experimental.pallas import tpu as pltpu
from jax.sharding import PartitionSpec as P

MESH = pl.DeviceIdType.MESH
F32 = jnp.float32
BF16 = jnp.bfloat16
LANES = 128


def iota(shape, axis):
    return lax.broadcasted_iota(jnp.int32, shape, axis)


def hot(mask):
    return jnp.where(mask, 1.0, 0.0).astype(BF16)


def nn(a, b):
    return jnp.dot(a, b, preferred_element_type=F32)


def nt(a, b):
    return lax.dot_general(a, b, (((1,), (1,)), ((), ())), preferred_element_type=F32)


def tn(a, b):
    return lax.dot_general(a, b, (((0,), (0,)), ((), ())), preferred_element_type=F32)


def column(row):
    return jnp.transpose(jnp.broadcast_to(row, (LANES, LANES)))


def each(count, body):
    if count <= 8:
        for step in range(count):
            body(step)
    else:
        lax.fori_loop(0, count, lambda step, _: (body(step), 0)[1], 0)


def kernel(
    dims,
    counts_hbm,
    entity_hbm,
    request_hbm,
    heads_hbm,
    rels_hbm,
    tails_hbm,
    negs_hbm,
    blocks_hbm,
    entity_out,
    relation_out,
    counts_ref,
    entity_ref,
    request_ref,
    heads_ref,
    rels_ref,
    tails_ref,
    negs_ref,
    blocks_ref,
    sum_a_ref,
    sum_b_ref,
    rel_out_ref,
    entity_stage,
    request_wide,
    request_send,
    request_recv,
    want_send,
    fetched,
    slot_send,
    scatter_hot,
    grads,
    tail_hot_t,
    codes,
    hot_rows,
    operators,
    operators_t,
    masked_heads,
    masked_grads,
    projected,
    neg_weight,
    neg_rows,
    weighted,
    pos_tail,
    grad_proj,
    grad_proj_t,
    part_send,
    part_recv,
    part_half,
    own_half,
    rel_send,
    rel_recv,
    rel_own,
    request_sems,
    fetch_sems,
    slot_sems,
    part_sems,
    cross_sems,
    near_sems,
    far_sems,
    rs_sems,
    ag_sems,
    in_sems,
    entity_sems,
    relation_sems,
):
    n_ent, n_rel = dims
    me, rel = lax.axis_index("ent"), lax.axis_index("rel")
    core, side = rel % 2, rel // 2
    near = side * 2 + (1 - core)
    cross = (1 - side) * 2 + core
    entities, width = entity_ref.shape
    slots = request_ref.shape[2]
    slot_total = n_ent * slots
    edges = heads_ref.shape[0] * LANES
    negs = negs_ref.shape[0] * LANES
    block = blocks_ref.shape[1]
    r_count = blocks_ref.shape[0] // width
    chunk = hot_rows.shape[0]
    chunks = edges // chunk
    piece = sum_a_ref.shape[2]
    per = LANES // slots
    head_bits = (entities - 1).bit_length()
    rel_bits = (r_count - 1).bit_length()
    neg_at, slot_at = edges, edges + negs
    half = entities // 2

    loads = [
        pltpu.make_async_copy(src, dst, in_sems.at[k])
        for k, (src, dst) in enumerate(
            (
                (request_hbm, request_ref),
                (heads_hbm, heads_ref),
                (rels_hbm, rels_ref),
                (tails_hbm, tails_ref),
                (negs_hbm, negs_ref),
                (entity_hbm, entity_ref),
                (blocks_hbm, blocks_ref),
                (counts_hbm, counts_ref),
            )
        )
    ]
    for load in loads:
        load.start()

    barrier = pltpu.get_barrier_semaphore()

    def greet(step):
        pl.semaphore_signal(
            barrier, inc=1, device_id=(lax.rem(me + step + 1, n_ent), rel), device_id_type=MESH
        )

    each(n_ent - 1, greet)
    for partner in (near, cross):
        pl.semaphore_signal(barrier, inc=1, device_id=(me, partner), device_id_type=MESH)

    request_wide[...] = jnp.zeros_like(request_wide)
    loads[0].wait()
    request_wide[:, :slots] = request_ref[0]
    base = request_wide[...]
    wide = base
    for q in range(1, per):
        wide = wide + pltpu.roll(base, q * slots, 1)
    for p in range(n_ent):
        request_send[p] = jnp.broadcast_to(wide[p : p + 1], (8, LANES))
    request_recv[me] = request_send[me]

    for load in loads[1:5]:
        load.wait()
    for k in range(edges // LANES):
        code = heads_ref[k : k + 1] + (
            (rels_ref[k : k + 1] + (tails_ref[k : k + 1] << rel_bits)) << head_bits
        )
        codes[k * LANES : (k + 1) * LANES] = column(code)
    lane = iota((LANES, LANES), 1)
    for k in range(negs // LANES):
        ids = column(negs_ref[k : k + 1])
        for c in range(entities // LANES):
            hot_rows[k * LANES : (k + 1) * LANES, c * LANES : (c + 1) * LANES] = hot(
                ids == lane + c * LANES
            )
    loads[5].wait()
    neg_rows[...] = nn(hot_rows[:negs], entity_ref[...]).astype(BF16)

    pl.semaphore_wait(barrier, n_ent + 1)

    def exchange(src, dst, sems, step):
        target = lax.rem(me + step + 1, n_ent)
        return pltpu.make_async_remote_copy(
            src_ref=src.at[target],
            dst_ref=dst.at[me],
            send_sem=sems.at[0, target],
            recv_sem=sems.at[1, me],
            device_id=(target, rel),
            device_id_type=MESH,
        )

    def arrival(dst, sems, step):
        source = lax.rem(me + step + 1, n_ent)
        return pltpu.make_async_remote_copy(
            src_ref=dst.at[source],
            dst_ref=dst.at[source],
            send_sem=sems.at[0, source],
            recv_sem=sems.at[1, source],
            device_id=(source, rel),
            device_id_type=MESH,
        )

    def start_all(src, dst, sems):
        each(n_ent - 1, lambda step: exchange(src, dst, sems, step).start())

    def wait_all(dst, sems):
        each(n_ent - 1, lambda step: arrival(dst, sems, step).wait_recv())

    def drain_all(src, dst, sems):
        each(n_ent - 1, lambda step: exchange(src, dst, sems, step).wait_send())

    start_all(request_send, request_recv, request_sems)

    spread = hot(iota((block, width), 1) % block == iota((block, width), 0))
    spread_t = hot(iota((width, block), 0) % block == iota((width, block), 1))
    diagonal = iota((width, width), 0) // block == iota((width, width), 1) // block
    loads[6].wait()
    loads[7].wait()
    live_count = counts_ref[0]
    for r in range(r_count):
        rows = slice(r * width, (r + 1) * width)
        one = blocks_ref[rows]
        plain = jnp.where(diagonal, nn(one, spread), 0.0).astype(BF16)
        turned = jnp.where(diagonal, nt(spread_t, one), 0.0).astype(BF16)
        for c in range(width // LANES):
            part = slice(c * LANES, (c + 1) * LANES)
            at = (c * r_count + r) * LANES
            operators[at : at + LANES] = plain[part]
            operators_t[at : at + LANES] = turned[part]

    def rel_masks(rows):
        ids = (codes[rows] >> head_bits) & (r_count - 1)
        return [hot(ids == r) for r in range(r_count)]

    def mask_by_rel(source, masks, target, rows):
        for r in range(r_count):
            for c in range(width // LANES):
                at = (c * r_count + r) * LANES
                target[rows, at : at + LANES] = source[:, c * LANES : (c + 1) * LANES] * masks[r]

    wide_lane = iota((chunk, LANES), 1)

    def project(i):
        rows = slice(i * chunk, (i + 1) * chunk)
        ids = codes[rows] & (entities - 1)
        for c in range(entities // LANES):
            hot_rows[:, c * LANES : (c + 1) * LANES] = hot(ids == wide_lane + c * LANES)
        head = nn(hot_rows[...], entity_ref[...]).astype(BF16)
        mask_by_rel(head, rel_masks(rows), masked_heads, rows)
        proj = nn(masked_heads[rows], operators[...]).astype(BF16)
        projected[rows] = proj
        score = nt(proj, neg_rows[...])
        live = iota((chunk, negs), 0) + i * chunk < live_count
        weight = jnp.where(live, jax.nn.sigmoid(score) * (1.0 / negs), 0.0).astype(BF16)
        neg_weight[rows] = weight
        return tn(weight, proj)

    neg_grad = project(0)

    wait_all(request_recv, request_sems)
    request_rows = []
    lane8 = iota((8, LANES), 1) // slots
    for g in range(n_ent // per):
        row = request_recv[g * per]
        for q in range(1, per):
            row = jnp.where(lane8 == q, request_recv[g * per + q], row)
        row = row[:1]
        request_rows.append(row)
        ids = column(row)
        for c in range(entities // LANES):
            hot_rows[:LANES, c * LANES : (c + 1) * LANES] = hot(ids == lane + c * LANES)
        want_send[g * per : (g + 1) * per] = (
            nn(hot_rows[:LANES], entity_ref[...]).astype(BF16).reshape(per, slots, width)
        )
    fetched[me] = want_send[me]
    start_all(want_send, fetched, fetch_sems)

    for i in range(1, chunks):
        neg_grad = neg_grad + project(i)
    grads[neg_at : neg_at + negs] = neg_grad.astype(BF16)

    sub = iota((entities, LANES), 0)
    for k in range(edges // LANES):
        scatter_hot[:, k * LANES : (k + 1) * LANES] = hot(sub == heads_ref[k : k + 1])
    for k in range(negs // LANES):
        at = neg_at + k * LANES
        scatter_hot[:, at : at + LANES] = hot(sub == negs_ref[k : k + 1])
    for k, row in enumerate(request_rows):
        at = slot_at + k * LANES
        scatter_hot[:, at : at + LANES] = hot(sub == row)
    slot_sub = iota((slot_total, LANES), 0)
    for k in range(edges // LANES):
        tail_hot_t[:, k * LANES : (k + 1) * LANES] = hot(slot_sub == tails_ref[k : k + 1])

    wait_all(fetched, fetch_sems)
    table = fetched[...].reshape(slot_total, width)
    for i in range(chunks):
        rows = slice(i * chunk, (i + 1) * chunk)
        ids = codes[rows] >> (head_bits + rel_bits)
        tail_hot = jnp.concatenate(
            [hot(ids == wide_lane + c * LANES) for c in range(slot_total // LANES)], axis=1
        )
        tail = nn(tail_hot, table)
        proj = projected[rows].astype(F32)
        positive = jnp.sum(proj * tail, axis=1, keepdims=True)
        live = iota((chunk, 1), 0) + i * chunk < live_count
        pos_weight = jnp.where(live, -jax.nn.sigmoid(-positive), 0.0)
        weighted[rows] = (pos_weight * proj).astype(BF16)
        pos_tail[rows] = pos_weight * tail
    per_step = min(n_ent, 8)
    for g in range(n_ent // per_step):
        rows = slice(g * per_step * slots, (g + 1) * per_step * slots)
        slot_send[g * per_step : (g + 1) * per_step] = (
            nn(tail_hot_t[rows], weighted[...]).astype(BF16).reshape(per_step, slots, width)
        )
    slot_recv = grads.at[slot_at : slot_at + slot_total]

    def slot_copy(step):
        target = lax.rem(me + step + 1, n_ent)
        return pltpu.make_async_remote_copy(
            src_ref=slot_send.at[target],
            dst_ref=grads.at[pl.ds(pl.multiple_of(slot_at + me * slots, slots), slots)],
            send_sem=slot_sems.at[0, target],
            recv_sem=slot_sems.at[1, me],
            device_id=(target, rel),
            device_id_type=MESH,
        )

    def slot_arrival(step):
        source = lax.rem(me + step + 1, n_ent)
        return pltpu.make_async_remote_copy(
            src_ref=slot_send.at[source],
            dst_ref=grads.at[pl.ds(pl.multiple_of(slot_at + source * slots, slots), slots)],
            send_sem=slot_sems.at[0, source],
            recv_sem=slot_sems.at[1, source],
            device_id=(source, rel),
            device_id_type=MESH,
        )

    each(n_ent - 1, lambda step: slot_copy(step).start())
    grads[pl.ds(pl.multiple_of(slot_at + me * slots, slots), slots)] = slot_send[me]

    for i in range(chunks):
        rows = slice(i * chunk, (i + 1) * chunk)
        grad_proj[rows] = (pos_tail[rows] + nn(neg_weight[rows], neg_rows[...])).astype(BF16)

    wire = rel_send.dtype
    per_owner = rel_send.shape[1]
    grad_proj_t[...] = jnp.transpose(grad_proj[...])
    step_rows = min(block, per_owner)
    span = r_count * LANES
    block_of_lane = iota((block, span), 1) // block % (LANES // block)
    for c in range(width // LANES):
        outer = nn(
            grad_proj_t[c * LANES : (c + 1) * LANES], masked_heads[:, c * span : (c + 1) * span]
        )
        small = jnp.zeros((block, span), F32)
        for n in range(LANES // block):
            small = jnp.where(block_of_lane == n, outer[n * block : (n + 1) * block], small)
        for r in range(r_count):
            for t in range(block // step_rows):
                flat = (r * (width // LANES) + c) * block + t * step_rows
                owner, at = flat // per_owner, flat % per_owner
                rel_send[owner, at : at + step_rows] = small[
                    t * step_rows : (t + 1) * step_rows, r * LANES : (r + 1) * LANES
                ].astype(wire)
    start_all(rel_send, rel_recv, rs_sems)
    rel_recv[me] = rel_send[me]

    for i in range(chunks):
        rows = slice(i * chunk, (i + 1) * chunk)
        mask_by_rel(grad_proj[rows], rel_masks(rows), masked_grads, rows)
    grads[:edges] = nn(masked_grads[...], operators_t[...]).astype(BF16)

    pieces = half // piece
    pair = pieces
    part_copies, cross_copies, near_copies, far_copies = [], [], [], []

    def near_copy(src, dst, sems, q, target):
        copy = pltpu.make_async_remote_copy(
            src_ref=src,
            dst_ref=dst,
            send_sem=sems.at[0, q],
            recv_sem=sems.at[1, q],
            device_id=(me, target),
            device_id_type=MESH,
        )
        copy.start()
        return copy

    def scatter(which, g, terms):
        at = pl.multiple_of(which * half + g * pair * piece, pair * piece)
        return nn(scatter_hot[pl.ds(at, pair * piece), terms], grads[terms])

    early, late = slice(0, slot_at), slice(slot_at, slot_at + slot_total)
    for g in range(pieces // pair):
        part_half[g] = scatter(1 - core, g, early)
        own_half[g] = scatter(core, g, early)
    each(n_ent - 1, lambda step: slot_arrival(step).wait_recv())
    for g in range(pieces // pair):
        part = (part_half[g] + scatter(1 - core, g, late)).astype(BF16)
        for q in range(g * pair, (g + 1) * pair):
            low = (q - g * pair) * piece
            part_send[q] = part[low : low + piece]
            part_copies.append(near_copy(part_send.at[q], part_recv.at[q], part_sems, q, near))
    for g in range(pieces // pair):
        own = own_half[g] + scatter(core, g, late)
        for q in range(g * pair, (g + 1) * pair):
            low = (q - g * pair) * piece
            part_copies[q].wait_recv()
            sum_a_ref[core, q] = (own[low : low + piece] + part_recv[q].astype(F32)).astype(BF16)
            mine = sum_a_ref.at[core, q]
            cross_copies.append(near_copy(mine, sum_b_ref.at[core, q], cross_sems, q, cross))
            near_copies.append(near_copy(mine, mine, near_sems, q, near))

    def write_entity(which, q):
        entity_stage[which, q] = sum_a_ref[which, q].astype(F32) + sum_b_ref[which, q].astype(F32)
        copy = pltpu.make_async_copy(
            entity_stage.at[which, q], entity_out.at[which, q], entity_sems.at[which, q]
        )
        copy.start()
        return copy

    wait_all(rel_recv, rs_sems)
    total = rel_recv[0].astype(F32)
    for p in range(1, n_ent):
        total = total + rel_recv[p].astype(F32)
    rel_own[...] = total.astype(wire)
    rel_out_ref[me] = rel_own[...]

    def gather_copy(step):
        target = lax.rem(me + step + 1, n_ent)
        return pltpu.make_async_remote_copy(
            src_ref=rel_own,
            dst_ref=rel_out_ref.at[me],
            send_sem=ag_sems.at[0, target],
            recv_sem=ag_sems.at[1, me],
            device_id=(target, rel),
            device_id_type=MESH,
        )

    each(n_ent - 1, lambda step: gather_copy(step).start())
    stores = []

    def forward(q):
        cross_copies[q].wait_recv()
        theirs = sum_b_ref.at[core, q]
        far_copies.append(near_copy(theirs, theirs, far_sems, q, near))
        stores.append(write_entity(core, q))

    def finish_other(q):
        near_copies[q].wait_recv()
        far_copies[q].wait_recv()
        stores.append(write_entity(1 - core, q))

    for q in range(pieces - 1):
        forward(q)
    wait_all(rel_out_ref, ag_sems)
    copy = pltpu.make_async_copy(rel_out_ref, relation_out, relation_sems.at[0])
    copy.start()
    stores.append(copy)
    for q in range(pieces - 1):
        finish_other(q)
    forward(pieces - 1)
    finish_other(pieces - 1)
    for copy in stores:
        copy.wait()
    drain_all(request_send, request_recv, request_sems)
    drain_all(want_send, fetched, fetch_sems)
    each(n_ent - 1, lambda step: slot_copy(step).wait_send())
    drain_all(rel_send, rel_recv, rs_sems)
    each(n_ent - 1, lambda step: gather_copy(step).wait_send())
    for copies in (part_copies, cross_copies, near_copies, far_copies):
        for copy in copies:
            copy.wait_send()


def finish(
    entity_ref, relation_ref, entity_out, relation_out, rel_in, rel_stage, stage, in_sems, out_sems
):
    count = out_sems.shape[1]
    rows = stage.shape[0] // count
    tall = rel_stage.shape[0] // count
    block = rel_stage.shape[1]
    rel_load = pltpu.make_async_copy(relation_ref, rel_in, in_sems.at[count])
    rel_load.start()
    loads, stores = [], []
    for c in range(count):
        at = pl.ds(c * rows, rows)
        loads.append(pltpu.make_async_copy(entity_ref.at[at], stage.at[at], in_sems.at[c]))
        loads[c].start()
    rel_load.wait()
    for c in range(count):
        for k in range(c * tall // LANES, (c + 1) * tall // LANES):
            rel_stage[k * LANES : (k + 1) * LANES] = jnp.transpose(
                rel_in[k * block : (k + 1) * block].astype(F32)
            )
        at = pl.ds(c * tall, tall)
        stores.append(
            pltpu.make_async_copy(rel_stage.at[at], relation_out.at[at], out_sems.at[1, c])
        )
        stores[-1].start()
    for c in range(count):
        loads[c].wait()
        at = pl.ds(c * rows, rows)
        stores.append(pltpu.make_async_copy(stage.at[at], entity_out.at[at], out_sems.at[0, c]))
        stores[-1].start()
    for store in stores:
        store.wait()


def local(
    n_ent,
    n_rel,
    entity_rows,
    request_rows,
    edge_heads,
    edge_rels,
    edge_tails,
    edge_counts,
    negative_rows,
    relation_blocks,
):
    entities, width = entity_rows.shape
    slots = request_rows.shape[2]
    slot_total = n_ent * slots
    edges = edge_heads.shape[0]
    negs = negative_rows.shape[0]
    r_count, block_count, block, _ = relation_blocks.shape
    chunk = min(512, edges)
    piece = 128
    pieces = entities // 2 // piece
    stacked = r_count * width
    flat_rows = stacked * block // LANES
    per_owner = flat_rows // n_ent
    wire = BF16 if per_owner % 16 == 0 else F32
    terms = edges + negs + slot_total
    vmem = pltpu.VMEM
    dma = pltpu.SemaphoreType.DMA
    spec = pl.BlockSpec(memory_space=pltpu.HBM)
    out_shape = (
        jax.ShapeDtypeStruct((2, pieces, piece, width), F32),
        jax.ShapeDtypeStruct((n_ent, per_owner, LANES), wire),
    )
    scratch = [
        pltpu.SMEM((1,), jnp.int32),
        vmem((entities, width), BF16),
        vmem(request_rows.shape, jnp.int32),
        vmem((edges // LANES, LANES), jnp.int32),
        vmem((edges // LANES, LANES), jnp.int32),
        vmem((edges // LANES, LANES), jnp.int32),
        vmem((negs // LANES, LANES), jnp.int32),
        vmem((stacked, block), BF16),
        vmem((2, pieces, piece, width), BF16),
        vmem((2, pieces, piece, width), BF16),
        vmem((n_ent, per_owner, LANES), wire),
        vmem((2, pieces, piece, width), F32),
        vmem((n_ent, LANES), jnp.int32),
        vmem((n_ent, 8, LANES), jnp.int32),
        vmem((n_ent, 8, LANES), jnp.int32),
        vmem((n_ent, slots, width), BF16),
        vmem((n_ent, slots, width), BF16),
        vmem((n_ent, slots, width), BF16),
        vmem((entities, terms), BF16),
        vmem((terms, width), BF16),
        vmem((slot_total, edges), BF16),
        vmem((edges, LANES), jnp.int32),
        vmem((chunk, entities), BF16),
        vmem((stacked, width), BF16),
        vmem((stacked, width), BF16),
        vmem((edges, stacked), BF16),
        vmem((edges, stacked), BF16),
        vmem((edges, width), BF16),
        vmem((edges, negs), BF16),
        vmem((negs, width), BF16),
        vmem((edges, width), BF16),
        vmem((edges, width), F32),
        vmem((edges, width), BF16),
        vmem((width, edges), BF16),
        vmem((pieces, piece, width), BF16),
        vmem((pieces, piece, width), BF16),
        vmem((1, pieces * piece, width), F32),
        vmem((1, pieces * piece, width), F32),
        vmem((n_ent, per_owner, LANES), wire),
        vmem((n_ent, per_owner, LANES), wire),
        vmem((per_owner, LANES), wire),
        dma((2, n_ent)),
        dma((2, n_ent)),
        dma((2, n_ent)),
        dma((2, pieces)),
        dma((2, pieces)),
        dma((2, pieces)),
        dma((2, pieces)),
        dma((2, n_ent)),
        dma((2, n_ent)),
        dma((8,)),
        dma((2, pieces)),
        dma((1,)),
    ]
    entity_sum, relation_sum = pl.pallas_call(
        functools.partial(kernel, (n_ent, n_rel)),
        out_shape=out_shape,
        in_specs=[spec] * 8,
        out_specs=(spec,) * 2,
        scratch_shapes=scratch,
        compiler_params=pltpu.CompilerParams(
            collective_id=0, has_side_effects=True, vmem_limit_bytes=56 * 1024 * 1024
        ),
    )(
        edge_counts,
        entity_rows,
        request_rows,
        edge_heads.reshape(edges // LANES, LANES),
        edge_rels.reshape(edges // LANES, LANES),
        edge_tails.reshape(edges // LANES, LANES),
        negative_rows.reshape(negs // LANES, LANES),
        relation_blocks.reshape(stacked, block),
    )
    entity_grad, relation_grad = pl.pallas_call(
        finish,
        out_shape=(
            jax.ShapeDtypeStruct((entities, width), F32),
            jax.ShapeDtypeStruct((stacked, block), F32),
        ),
        in_specs=[spec] * 2,
        out_specs=(spec,) * 2,
        scratch_shapes=[
            vmem((flat_rows, LANES), wire),
            vmem((stacked, block), F32),
            vmem((entities, width), F32),
            dma((9,)),
            dma((2, 8)),
        ],
        compiler_params=pltpu.CompilerParams(vmem_limit_bytes=56 * 1024 * 1024),
    )(entity_sum.reshape(entities, width), relation_sum.reshape(flat_rows, LANES))
    return entity_grad, relation_grad.reshape(relation_blocks.shape)


def solution(mesh):
    in_specs = (
        P("ent", None),
        P("ent", None, None),
        P(("ent", "rel")),
        P(("ent", "rel")),
        P(("ent", "rel")),
        P(("ent", "rel")),
        P(("ent", "rel")),
        P("rel", None, None, None),
    )
    out_specs = (P("ent", None), P("rel", None, None, None))
    body = functools.partial(local, mesh.shape["ent"], mesh.shape["rel"])
    return jax.shard_map(body, mesh=mesh, in_specs=in_specs, out_specs=out_specs, check_vma=False)
```

```python
import functools

import jax
import jax.numpy as jnp
from jax import lax
from jax.experimental import pallas as pl
from jax.experimental.pallas import tpu as pltpu
from jax.sharding import PartitionSpec as P

MESH = pl.DeviceIdType.MESH
F32 = jnp.float32
BF16 = jnp.bfloat16
LANES = 128


def iota(shape, axis):
    return lax.broadcasted_iota(jnp.int32, shape, axis)


def hot(mask):
    return jnp.where(mask, 1.0, 0.0).astype(BF16)


def nn(a, b):
    return jnp.dot(a, b, preferred_element_type=F32)


def nt(a, b):
    return lax.dot_general(a, b, (((1,), (1,)), ((), ())), preferred_element_type=F32)


def tn(a, b):
    return lax.dot_general(a, b, (((0,), (0,)), ((), ())), preferred_element_type=F32)


def column(row):
    return jnp.transpose(jnp.broadcast_to(row, (LANES, LANES)))


def each(count, body):
    if count <= 8:
        for step in range(count):
            body(step)
    else:
        lax.fori_loop(0, count, lambda step, _: (body(step), 0)[1], 0)


def kernel(
    dims,
    counts_hbm,
    entity_hbm,
    request_hbm,
    heads_hbm,
    rels_hbm,
    tails_hbm,
    negs_hbm,
    blocks_hbm,
    entity_out,
    relation_out,
    counts_ref,
    entity_ref,
    request_ref,
    heads_ref,
    rels_ref,
    tails_ref,
    negs_ref,
    blocks_ref,
    sum_a_ref,
    sum_b_ref,
    rel_out_ref,
    entity_stage,
    request_wide,
    request_send,
    request_recv,
    want_send,
    fetched,
    slot_send,
    scatter_hot,
    grads,
    tail_hot_t,
    codes,
    hot_rows,
    operators,
    operators_t,
    masked_heads,
    masked_grads,
    projected,
    neg_weight,
    neg_rows,
    weighted,
    pos_tail,
    grad_proj,
    grad_proj_t,
    part_send,
    part_recv,
    part_half,
    own_half,
    rel_send,
    rel_recv,
    rel_own,
    request_sems,
    fetch_sems,
    slot_sems,
    part_sems,
    cross_sems,
    near_sems,
    far_sems,
    rs_sems,
    ag_sems,
    in_sems,
    entity_sems,
    relation_sems,
):
    n_ent, n_rel = dims
    me, rel = lax.axis_index("ent"), lax.axis_index("rel")
    core, side = rel % 2, rel // 2
    near = side * 2 + (1 - core)
    cross = (1 - side) * 2 + core
    entities, width = entity_ref.shape
    slots = request_ref.shape[2]
    slot_total = n_ent * slots
    edges = heads_ref.shape[0] * LANES
    negs = negs_ref.shape[0] * LANES
    block = blocks_ref.shape[1]
    r_count = blocks_ref.shape[0] // width
    chunk = hot_rows.shape[0]
    chunks = edges // chunk
    piece = sum_a_ref.shape[2]
    per = LANES // slots
    head_bits = (entities - 1).bit_length()
    rel_bits = (r_count - 1).bit_length()
    neg_at, slot_at = edges, edges + negs
    half = entities // 2

    loads = [
        pltpu.make_async_copy(src, dst, in_sems.at[k])
        for k, (src, dst) in enumerate(
            (
                (request_hbm, request_ref),
                (heads_hbm, heads_ref),
                (rels_hbm, rels_ref),
                (tails_hbm, tails_ref),
                (negs_hbm, negs_ref),
                (entity_hbm, entity_ref),
                (blocks_hbm, blocks_ref),
                (counts_hbm, counts_ref),
            )
        )
    ]
    for load in loads:
        load.start()

    barrier = pltpu.get_barrier_semaphore()

    def greet(step):
        pl.semaphore_signal(
            barrier, inc=1, device_id=(lax.rem(me + step + 1, n_ent), rel), device_id_type=MESH
        )

    each(n_ent - 1, greet)
    for partner in (near, cross):
        pl.semaphore_signal(barrier, inc=1, device_id=(me, partner), device_id_type=MESH)

    request_wide[...] = jnp.zeros_like(request_wide)
    loads[0].wait()
    request_wide[:, :slots] = request_ref[0]
    base = request_wide[...]
    wide = base
    for q in range(1, per):
        wide = wide + pltpu.roll(base, q * slots, 1)
    for p in range(n_ent):
        request_send[p] = jnp.broadcast_to(wide[p : p + 1], (8, LANES))
    request_recv[me] = request_send[me]

    for load in loads[1:5]:
        load.wait()
    for k in range(edges // LANES):
        code = heads_ref[k : k + 1] + (
            (rels_ref[k : k + 1] + (tails_ref[k : k + 1] << rel_bits)) << head_bits
        )
        codes[k * LANES : (k + 1) * LANES] = column(code)
    lane = iota((LANES, LANES), 1)
    for k in range(negs // LANES):
        ids = column(negs_ref[k : k + 1])
        for c in range(entities // LANES):
            hot_rows[k * LANES : (k + 1) * LANES, c * LANES : (c + 1) * LANES] = hot(
                ids == lane + c * LANES
            )
    loads[5].wait()
    neg_rows[...] = nn(hot_rows[:negs], entity_ref[...]).astype(BF16)

    pl.semaphore_wait(barrier, n_ent + 1)

    def exchange(src, dst, sems, step):
        target = lax.rem(me + step + 1, n_ent)
        return pltpu.make_async_remote_copy(
            src_ref=src.at[target],
            dst_ref=dst.at[me],
            send_sem=sems.at[0, target],
            recv_sem=sems.at[1, me],
            device_id=(target, rel),
            device_id_type=MESH,
        )

    def arrival(dst, sems, step):
        source = lax.rem(me + step + 1, n_ent)
        return pltpu.make_async_remote_copy(
            src_ref=dst.at[source],
            dst_ref=dst.at[source],
            send_sem=sems.at[0, source],
            recv_sem=sems.at[1, source],
            device_id=(source, rel),
            device_id_type=MESH,
        )

    def start_all(src, dst, sems):
        each(n_ent - 1, lambda step: exchange(src, dst, sems, step).start())

    def wait_all(dst, sems):
        each(n_ent - 1, lambda step: arrival(dst, sems, step).wait_recv())

    def drain_all(src, dst, sems):
        each(n_ent - 1, lambda step: exchange(src, dst, sems, step).wait_send())

    start_all(request_send, request_recv, request_sems)

    spread = hot(iota((block, width), 1) % block == iota((block, width), 0))
    spread_t = hot(iota((width, block), 0) % block == iota((width, block), 1))
    diagonal = iota((width, width), 0) // block == iota((width, width), 1) // block
    loads[6].wait()
    loads[7].wait()
    live_count = counts_ref[0]
    for r in range(r_count):
        rows = slice(r * width, (r + 1) * width)
        one = blocks_ref[rows]
        plain = jnp.where(diagonal, nn(one, spread), 0.0).astype(BF16)
        turned = jnp.where(diagonal, nt(spread_t, one), 0.0).astype(BF16)
        for c in range(width // LANES):
            part = slice(c * LANES, (c + 1) * LANES)
            at = (c * r_count + r) * LANES
            operators[at : at + LANES] = plain[part]
            operators_t[at : at + LANES] = turned[part]

    def rel_masks(rows):
        ids = (codes[rows] >> head_bits) & (r_count - 1)
        return [hot(ids == r) for r in range(r_count)]

    def mask_by_rel(source, masks, target, rows):
        for r in range(r_count):
            for c in range(width // LANES):
                at = (c * r_count + r) * LANES
                target[rows, at : at + LANES] = source[:, c * LANES : (c + 1) * LANES] * masks[r]

    wide_lane = iota((chunk, LANES), 1)

    def project(i):
        rows = slice(i * chunk, (i + 1) * chunk)
        ids = codes[rows] & (entities - 1)
        for c in range(entities // LANES):
            hot_rows[:, c * LANES : (c + 1) * LANES] = hot(ids == wide_lane + c * LANES)
        head = nn(hot_rows[...], entity_ref[...]).astype(BF16)
        mask_by_rel(head, rel_masks(rows), masked_heads, rows)
        proj = nn(masked_heads[rows], operators[...]).astype(BF16)
        projected[rows] = proj
        score = nt(proj, neg_rows[...])
        live = iota((chunk, negs), 0) + i * chunk < live_count
        weight = jnp.where(live, jax.nn.sigmoid(score) * (1.0 / negs), 0.0).astype(BF16)
        neg_weight[rows] = weight
        return tn(weight, proj)

    sub = iota((entities, LANES), 0)
    for k in range(edges // LANES):
        scatter_hot[:, k * LANES : (k + 1) * LANES] = hot(sub == heads_ref[k : k + 1])
    for k in range(negs // LANES):
        at = neg_at + k * LANES
        scatter_hot[:, at : at + LANES] = hot(sub == negs_ref[k : k + 1])
    slot_sub = iota((slot_total, LANES), 0)
    for k in range(edges // LANES):
        tail_hot_t[:, k * LANES : (k + 1) * LANES] = hot(slot_sub == tails_ref[k : k + 1])

    wait_all(request_recv, request_sems)
    request_rows = []
    lane8 = iota((8, LANES), 1) // slots
    for g in range(n_ent // per):
        row = request_recv[g * per]
        for q in range(1, per):
            row = jnp.where(lane8 == q, request_recv[g * per + q], row)
        row = row[:1]
        request_rows.append(row)
        ids = column(row)
        for c in range(entities // LANES):
            hot_rows[:LANES, c * LANES : (c + 1) * LANES] = hot(ids == lane + c * LANES)
        want_send[g * per : (g + 1) * per] = (
            nn(hot_rows[:LANES], entity_ref[...]).astype(BF16).reshape(per, slots, width)
        )
    fetched[me] = want_send[me]
    start_all(want_send, fetched, fetch_sems)

    neg_grad = project(0)
    for i in range(1, chunks):
        neg_grad = neg_grad + project(i)
    grads[neg_at : neg_at + negs] = neg_grad.astype(BF16)

    for k, row in enumerate(request_rows):
        at = slot_at + k * LANES
        scatter_hot[:, at : at + LANES] = hot(sub == row)

    wait_all(fetched, fetch_sems)
    table = fetched[...].reshape(slot_total, width)
    for i in range(chunks):
        rows = slice(i * chunk, (i + 1) * chunk)
        ids = codes[rows] >> (head_bits + rel_bits)
        tail_hot = jnp.concatenate(
            [hot(ids == wide_lane + c * LANES) for c in range(slot_total // LANES)], axis=1
        )
        tail = nn(tail_hot, table)
        proj = projected[rows].astype(F32)
        positive = jnp.sum(proj * tail, axis=1, keepdims=True)
        live = iota((chunk, 1), 0) + i * chunk < live_count
        pos_weight = jnp.where(live, -jax.nn.sigmoid(-positive), 0.0)
        weighted[rows] = (pos_weight * proj).astype(BF16)
        pos_tail[rows] = pos_weight * tail
    per_step = min(n_ent, 8)
    for g in range(n_ent // per_step):
        rows = slice(g * per_step * slots, (g + 1) * per_step * slots)
        slot_send[g * per_step : (g + 1) * per_step] = (
            nn(tail_hot_t[rows], weighted[...]).astype(BF16).reshape(per_step, slots, width)
        )
    slot_recv = grads.at[slot_at : slot_at + slot_total]

    def slot_copy(step):
        target = lax.rem(me + step + 1, n_ent)
        return pltpu.make_async_remote_copy(
            src_ref=slot_send.at[target],
            dst_ref=grads.at[pl.ds(pl.multiple_of(slot_at + me * slots, slots), slots)],
            send_sem=slot_sems.at[0, target],
            recv_sem=slot_sems.at[1, me],
            device_id=(target, rel),
            device_id_type=MESH,
        )

    def slot_arrival(step):
        source = lax.rem(me + step + 1, n_ent)
        return pltpu.make_async_remote_copy(
            src_ref=slot_send.at[source],
            dst_ref=grads.at[pl.ds(pl.multiple_of(slot_at + source * slots, slots), slots)],
            send_sem=slot_sems.at[0, source],
            recv_sem=slot_sems.at[1, source],
            device_id=(source, rel),
            device_id_type=MESH,
        )

    each(n_ent - 1, lambda step: slot_copy(step).start())
    grads[pl.ds(pl.multiple_of(slot_at + me * slots, slots), slots)] = slot_send[me]

    for i in range(chunks):
        rows = slice(i * chunk, (i + 1) * chunk)
        grad_proj[rows] = (pos_tail[rows] + nn(neg_weight[rows], neg_rows[...])).astype(BF16)

    wire = rel_send.dtype
    per_owner = rel_send.shape[1]
    grad_proj_t[...] = jnp.transpose(grad_proj[...])
    step_rows = min(block, per_owner)
    span = r_count * LANES
    block_of_lane = iota((block, span), 1) // block % (LANES // block)
    for c in range(width // LANES):
        outer = nn(
            grad_proj_t[c * LANES : (c + 1) * LANES], masked_heads[:, c * span : (c + 1) * span]
        )
        small = jnp.zeros((block, span), F32)
        for n in range(LANES // block):
            small = jnp.where(block_of_lane == n, outer[n * block : (n + 1) * block], small)
        for r in range(r_count):
            for t in range(block // step_rows):
                flat = (r * (width // LANES) + c) * block + t * step_rows
                owner, at = flat // per_owner, flat % per_owner
                rel_send[owner, at : at + step_rows] = small[
                    t * step_rows : (t + 1) * step_rows, r * LANES : (r + 1) * LANES
                ].astype(wire)
    start_all(rel_send, rel_recv, rs_sems)
    rel_recv[me] = rel_send[me]

    for i in range(chunks):
        rows = slice(i * chunk, (i + 1) * chunk)
        mask_by_rel(grad_proj[rows], rel_masks(rows), masked_grads, rows)
    grads[:edges] = nn(masked_grads[...], operators_t[...]).astype(BF16)

    pieces = half // piece
    pair = pieces
    part_copies, cross_copies, near_copies, far_copies = [], [], [], []

    def near_copy(src, dst, sems, q, target):
        copy = pltpu.make_async_remote_copy(
            src_ref=src,
            dst_ref=dst,
            send_sem=sems.at[0, q],
            recv_sem=sems.at[1, q],
            device_id=(me, target),
            device_id_type=MESH,
        )
        copy.start()
        return copy

    def scatter(which, g, terms):
        at = pl.multiple_of(which * half + g * pair * piece, pair * piece)
        return nn(scatter_hot[pl.ds(at, pair * piece), terms], grads[terms])

    early, late = slice(0, slot_at), slice(slot_at, slot_at + slot_total)
    for g in range(pieces // pair):
        part_half[g] = scatter(1 - core, g, early)
        own_half[g] = scatter(core, g, early)
    each(n_ent - 1, lambda step: slot_arrival(step).wait_recv())
    for g in range(pieces // pair):
        part = (part_half[g] + scatter(1 - core, g, late)).astype(BF16)
        for q in range(g * pair, (g + 1) * pair):
            low = (q - g * pair) * piece
            part_send[q] = part[low : low + piece]
            part_copies.append(near_copy(part_send.at[q], part_recv.at[q], part_sems, q, near))
    for g in range(pieces // pair):
        own = own_half[g] + scatter(core, g, late)
        for q in range(g * pair, (g + 1) * pair):
            low = (q - g * pair) * piece
            part_copies[q].wait_recv()
            sum_a_ref[core, q] = (own[low : low + piece] + part_recv[q].astype(F32)).astype(BF16)
            mine = sum_a_ref.at[core, q]
            cross_copies.append(near_copy(mine, sum_b_ref.at[core, q], cross_sems, q, cross))
            near_copies.append(near_copy(mine, mine, near_sems, q, near))

    def write_entity(which, q):
        entity_stage[which, q] = sum_a_ref[which, q].astype(F32) + sum_b_ref[which, q].astype(F32)
        copy = pltpu.make_async_copy(
            entity_stage.at[which, q], entity_out.at[which, q], entity_sems.at[which, q]
        )
        copy.start()
        return copy

    wait_all(rel_recv, rs_sems)
    total = rel_recv[0].astype(F32)
    for p in range(1, n_ent):
        total = total + rel_recv[p].astype(F32)
    rel_own[...] = total.astype(wire)
    rel_out_ref[me] = rel_own[...]

    def gather_copy(step):
        target = lax.rem(me + step + 1, n_ent)
        return pltpu.make_async_remote_copy(
            src_ref=rel_own,
            dst_ref=rel_out_ref.at[me],
            send_sem=ag_sems.at[0, target],
            recv_sem=ag_sems.at[1, me],
            device_id=(target, rel),
            device_id_type=MESH,
        )

    each(n_ent - 1, lambda step: gather_copy(step).start())
    stores = []

    def forward(q):
        cross_copies[q].wait_recv()
        theirs = sum_b_ref.at[core, q]
        far_copies.append(near_copy(theirs, theirs, far_sems, q, near))
        stores.append(write_entity(core, q))

    def finish_other(q):
        near_copies[q].wait_recv()
        far_copies[q].wait_recv()
        stores.append(write_entity(1 - core, q))

    for q in range(pieces - 1):
        forward(q)
    wait_all(rel_out_ref, ag_sems)
    copy = pltpu.make_async_copy(rel_out_ref, relation_out, relation_sems.at[0])
    copy.start()
    stores.append(copy)
    for q in range(pieces - 1):
        finish_other(q)
    forward(pieces - 1)
    finish_other(pieces - 1)
    for copy in stores:
        copy.wait()
    drain_all(request_send, request_recv, request_sems)
    drain_all(want_send, fetched, fetch_sems)
    each(n_ent - 1, lambda step: slot_copy(step).wait_send())
    drain_all(rel_send, rel_recv, rs_sems)
    each(n_ent - 1, lambda step: gather_copy(step).wait_send())
    for copies in (part_copies, cross_copies, near_copies, far_copies):
        for copy in copies:
            copy.wait_send()


def finish(
    entity_ref, relation_ref, entity_out, relation_out, rel_in, rel_stage, stage, in_sems, out_sems
):
    count = out_sems.shape[1]
    rows = stage.shape[0] // count
    tall = rel_stage.shape[0] // count
    block = rel_stage.shape[1]
    rel_load = pltpu.make_async_copy(relation_ref, rel_in, in_sems.at[count])
    rel_load.start()
    loads, stores = [], []
    for c in range(count):
        at = pl.ds(c * rows, rows)
        loads.append(pltpu.make_async_copy(entity_ref.at[at], stage.at[at], in_sems.at[c]))
        loads[c].start()
    rel_load.wait()
    for c in range(count):
        for k in range(c * tall // LANES, (c + 1) * tall // LANES):
            rel_stage[k * LANES : (k + 1) * LANES] = jnp.transpose(
                rel_in[k * block : (k + 1) * block].astype(F32)
            )
        at = pl.ds(c * tall, tall)
        stores.append(
            pltpu.make_async_copy(rel_stage.at[at], relation_out.at[at], out_sems.at[1, c])
        )
        stores[-1].start()
    for c in range(count):
        loads[c].wait()
        at = pl.ds(c * rows, rows)
        stores.append(pltpu.make_async_copy(stage.at[at], entity_out.at[at], out_sems.at[0, c]))
        stores[-1].start()
    for store in stores:
        store.wait()


def local(
    n_ent,
    n_rel,
    entity_rows,
    request_rows,
    edge_heads,
    edge_rels,
    edge_tails,
    edge_counts,
    negative_rows,
    relation_blocks,
):
    entities, width = entity_rows.shape
    slots = request_rows.shape[2]
    slot_total = n_ent * slots
    edges = edge_heads.shape[0]
    negs = negative_rows.shape[0]
    r_count, block_count, block, _ = relation_blocks.shape
    chunk = min(512, edges)
    piece = 128
    pieces = entities // 2 // piece
    stacked = r_count * width
    flat_rows = stacked * block // LANES
    per_owner = flat_rows // n_ent
    wire = BF16 if per_owner % 16 == 0 else F32
    terms = edges + negs + slot_total
    vmem = pltpu.VMEM
    dma = pltpu.SemaphoreType.DMA
    spec = pl.BlockSpec(memory_space=pltpu.HBM)
    out_shape = (
        jax.ShapeDtypeStruct((2, pieces, piece, width), F32),
        jax.ShapeDtypeStruct((n_ent, per_owner, LANES), wire),
    )
    scratch = [
        pltpu.SMEM((1,), jnp.int32),
        vmem((entities, width), BF16),
        vmem(request_rows.shape, jnp.int32),
        vmem((edges // LANES, LANES), jnp.int32),
        vmem((edges // LANES, LANES), jnp.int32),
        vmem((edges // LANES, LANES), jnp.int32),
        vmem((negs // LANES, LANES), jnp.int32),
        vmem((stacked, block), BF16),
        vmem((2, pieces, piece, width), BF16),
        vmem((2, pieces, piece, width), BF16),
        vmem((n_ent, per_owner, LANES), wire),
        vmem((2, pieces, piece, width), F32),
        vmem((n_ent, LANES), jnp.int32),
        vmem((n_ent, 8, LANES), jnp.int32),
        vmem((n_ent, 8, LANES), jnp.int32),
        vmem((n_ent, slots, width), BF16),
        vmem((n_ent, slots, width), BF16),
        vmem((n_ent, slots, width), BF16),
        vmem((entities, terms), BF16),
        vmem((terms, width), BF16),
        vmem((slot_total, edges), BF16),
        vmem((edges, LANES), jnp.int32),
        vmem((chunk, entities), BF16),
        vmem((stacked, width), BF16),
        vmem((stacked, width), BF16),
        vmem((edges, stacked), BF16),
        vmem((edges, stacked), BF16),
        vmem((edges, width), BF16),
        vmem((edges, negs), BF16),
        vmem((negs, width), BF16),
        vmem((edges, width), BF16),
        vmem((edges, width), F32),
        vmem((edges, width), BF16),
        vmem((width, edges), BF16),
        vmem((pieces, piece, width), BF16),
        vmem((pieces, piece, width), BF16),
        vmem((1, pieces * piece, width), F32),
        vmem((1, pieces * piece, width), F32),
        vmem((n_ent, per_owner, LANES), wire),
        vmem((n_ent, per_owner, LANES), wire),
        vmem((per_owner, LANES), wire),
        dma((2, n_ent)),
        dma((2, n_ent)),
        dma((2, n_ent)),
        dma((2, pieces)),
        dma((2, pieces)),
        dma((2, pieces)),
        dma((2, pieces)),
        dma((2, n_ent)),
        dma((2, n_ent)),
        dma((8,)),
        dma((2, pieces)),
        dma((1,)),
    ]
    entity_sum, relation_sum = pl.pallas_call(
        functools.partial(kernel, (n_ent, n_rel)),
        out_shape=out_shape,
        in_specs=[spec] * 8,
        out_specs=(spec,) * 2,
        scratch_shapes=scratch,
        compiler_params=pltpu.CompilerParams(
            collective_id=0, has_side_effects=True, vmem_limit_bytes=56 * 1024 * 1024
        ),
    )(
        edge_counts,
        entity_rows,
        request_rows,
        edge_heads.reshape(edges // LANES, LANES),
        edge_rels.reshape(edges // LANES, LANES),
        edge_tails.reshape(edges // LANES, LANES),
        negative_rows.reshape(negs // LANES, LANES),
        relation_blocks.reshape(stacked, block),
    )
    entity_grad, relation_grad = pl.pallas_call(
        finish,
        out_shape=(
            jax.ShapeDtypeStruct((entities, width), F32),
            jax.ShapeDtypeStruct((stacked, block), F32),
        ),
        in_specs=[spec] * 2,
        out_specs=(spec,) * 2,
        scratch_shapes=[
            vmem((flat_rows, LANES), wire),
            vmem((stacked, block), F32),
            vmem((entities, width), F32),
            dma((9,)),
            dma((2, 8)),
        ],
        compiler_params=pltpu.CompilerParams(vmem_limit_bytes=56 * 1024 * 1024),
    )(entity_sum.reshape(entities, width), relation_sum.reshape(flat_rows, LANES))
    return entity_grad, relation_grad.reshape(relation_blocks.shape)


def solution(mesh):
    in_specs = (
        P("ent", None),
        P("ent", None, None),
        P(("ent", "rel")),
        P(("ent", "rel")),
        P(("ent", "rel")),
        P(("ent", "rel")),
        P(("ent", "rel")),
        P("rel", None, None, None),
    )
    out_specs = (P("ent", None), P("rel", None, None, None))
    body = functools.partial(local, mesh.shape["ent"], mesh.shape["rel"])
    return jax.shard_map(body, mesh=mesh, in_specs=in_specs, out_specs=out_specs, check_vma=False)
```
